128 devices in a mesh: dp: 8 (over y, core), expert: 16 (over z, x).
Axes of the slice: x: 4, y: 4, z: 4, core: 2. Of those that a mesh axis runs over, the one named last changes fastest.
Arguments:
- tokens: bfloat16 [16384, 4096], P(('dp', 'expert')), may hold values from -6 to 6
- expert_ids: int32 [16384, 4], P(('dp', 'expert')), may hold values from 0 to 15, as said below
- gate_values: float32 [16384, 4], P(('dp', 'expert')), may hold values from 0.1 to 1
- gate_weight: bfloat16 [16, 4096, 768], P('expert'), may hold values from -0.09375 to 0.09375
- up_weight: bfloat16 [16, 4096, 768], P('expert'), may hold values from -0.09375 to 0.09375
- down_weight: bfloat16 [16, 768, 4096], P('expert'), may hold values from -0.21875 to 0.21875
Outputs:
- mixed: bfloat16 [16384, 4096], P(('dp', 'expert'))
The draws below stay inside these ranges and needn't reach their ends.
Inputs may be any that keep to these rules, and one draw needn't show every extreme that they name: `expert_ids`: each token names 4 different experts; at most 64 tokens of one device name one expert, and on every device exactly one expert is named by 64 of its tokens, the same expert for all devices of one index of dp.
All inputs are finite; a program needn't handle non-finite values.
Results may differ from the reference program's by a relative error of at most 0.0058.
Values may be sent and summed in bfloat16 or wider, within the bound.
No kernel may reach another device: no remote copies, remote signals or barrier semaphores. Data moves between devices by JAX's collectives and lax.ppermute only.
A program may use at most 128 MiB of HBM per device.

```python
import math
import jax
import jax.numpy as jnp
from jax import lax

D = 4096
FF = 768
TOK_DEV = 128
TOP = 4
EXPERTS = 16
TOKENS = 16384
CAP = 64


def draw_expert_ids(key, part):
    key = jax.random.fold_in(key, 7)
    blocks_all = TOKENS // TOK_DEV
    entries = TOK_DEV * TOP
    rest_total = entries - CAP
    others_count = EXPERTS - 1
    base_load = rest_total // others_count
    extra_ones = rest_total % others_count
    spread = base_load // 2
    pair_count = others_count // 2

    def one_block(block):
        block_key = jax.random.fold_in(key, block)
        row_key = jax.random.fold_in(key, block // EXPERTS + 1000003)
        hottest = jax.random.randint(row_key, (), 0, EXPERTS)
        order = jax.random.permutation(jax.random.fold_in(block_key, 1), others_count)
        others = order + (order >= hottest).astype(jnp.int32)
        loads = base_load + (jnp.arange(others_count) < extra_ones).astype(jnp.int32)
        shifts = jax.random.randint(jax.random.fold_in(block_key, 2), (pair_count,), -spread, spread + 1)
        change = jnp.zeros(others_count, jnp.int32)
        change = change.at[0:2 * pair_count:2].add(shifts).at[1:2 * pair_count:2].add(-shifts)
        loads = loads + change
        counts = jnp.zeros(EXPERTS, jnp.int32).at[others].set(loads).at[hottest].set(CAP)
        bounds = jnp.cumsum(counts)
        listing = jnp.sum((bounds[None, :] <= jnp.arange(entries)[:, None]).astype(jnp.int32), axis=1)
        chosen = listing.reshape(TOP, TOK_DEV).T
        mixing = jax.random.permutation(jax.random.fold_in(block_key, 3), TOK_DEV)
        return chosen[mixing]
    return jax.vmap(one_block)(jnp.arange(blocks_all)).reshape(TOKENS, TOP).astype(jnp.int32)


def block_levels(own_key, dims, shards, low, top_value):
    def one(dim, parts):
        heights = jax.random.uniform(jax.random.fold_in(jax.random.fold_in(own_key, 6), dim), (parts,), jnp.float32, low / len(shards), top_value / len(shards))
        return jnp.repeat(jnp.exp(heights), dims[dim] // parts).reshape((-1,) + (1,) * (len(dims) - dim - 1))

    loudness = one(*shards[0])
    for cut in shards[1:]:
        loudness = loudness * one(*cut)
    return loudness


def bell_draw(own_key, extent, deviation, reach, cuts=(), dtype=jnp.bfloat16):
    gain = block_levels(own_key, extent, cuts, -0.22, 0.18) if cuts else 1.0
    values = jax.random.normal(own_key, extent, jnp.float32) * deviation * gain
    return jnp.minimum(jnp.maximum(values, -reach), reach).astype(dtype)


def setup_inputs(seed: int = 0) -> dict:
    arg_keys = jax.random.split(jax.random.key(seed), 7)
    return {
        "tokens": bell_draw(arg_keys[0], (TOKENS, D), 1.0, 6.0, ((0, 128),)),
        "expert_ids": draw_expert_ids(jax.random.fold_in(arg_keys[6], 71), 0),
        "gate_values": jnp.clip(jnp.exp(math.log(1.0) - 2.3025851 * jax.random.uniform(arg_keys[2], (TOKENS, TOP), jnp.float32) ** block_levels(arg_keys[2], (TOKENS, TOP), ((0, 128),), -0.2, 0.2)), 0.1, 1.0),
        "gate_weight": bell_draw(arg_keys[3], (EXPERTS, D, FF), D ** -0.5, 0.09375, ((0, 16),)),
        "up_weight": bell_draw(arg_keys[4], (EXPERTS, D, FF), D ** -0.5, 0.09375, ((0, 16),)),
        "down_weight": bell_draw(arg_keys[5], (EXPERTS, FF, D), FF ** -0.5, 0.21875, ((0, 16),)),
    }


def expert_rows(rows, w_gate, w_up, w_down):
    gate_part = jnp.dot(rows, w_gate, preferred_element_type=jnp.float32)
    up_part = jnp.dot(rows, w_up, preferred_element_type=jnp.float32)
    hidden = (jax.nn.silu(gate_part) * up_part).astype(jnp.bfloat16)
    return jnp.dot(hidden, w_down, preferred_element_type=jnp.float32).astype(jnp.bfloat16)


def reference(tokens, expert_ids, gate_values, gate_weight, up_weight, down_weight):
    most_rows = (TOKENS // TOK_DEV) * CAP

    def per_expert(expert, mixed_sum):
        picked = expert_ids == expert
        weight_sum = jnp.sum(jnp.where(picked, gate_values, jnp.zeros_like(gate_values)), axis=1)
        chosen_any = jnp.any(picked, axis=1)
        index = jnp.nonzero(chosen_any, size=most_rows, fill_value=TOKENS)[0]
        safe = jnp.minimum(index, TOKENS - 1)
        outputs = expert_rows(tokens[safe], gate_weight[expert], up_weight[expert], down_weight[expert])
        scales = jnp.where(index < TOKENS, weight_sum[safe], jnp.zeros_like(weight_sum[safe]))
        return mixed_sum.at[index].add(scales[:, None] * outputs.astype(jnp.float32), mode="drop")

    total = lax.fori_loop(0, EXPERTS, per_expert, jnp.zeros((TOKENS, D), jnp.float32))
    return total.astype(jnp.bfloat16)
```

```python
import functools

import jax
import jax.numpy as jnp
from jax import lax
from jax.experimental import pallas as pl
from jax.experimental.pallas import tpu as pltpu
from jax.sharding import Mesh, PartitionSpec as P

SIDE = 4
CAP = 64
CHUNKS = 2
ROWS = CAP // CHUNKS
PACK_TILE = 512
FF_TILE = 256
D_TILE = 512
SUM_TILE = 512
VMEM = 50 * 1024 * 1024


def shift(block, axis, step):
    return lax.ppermute(block, axis, [(i, (i + step) % SIDE) for i in range(SIDE)])


def slots_of(ids, expert):
    named = jnp.any(ids == expert[..., None, None], axis=-2)
    tokens = ids.shape[-1]
    before = (jnp.arange(tokens)[:, None] < jnp.arange(tokens)[None, :]).astype(jnp.bfloat16)
    rank = jnp.dot(named.astype(jnp.bfloat16), before, preferred_element_type=jnp.float32)
    return jnp.where(named, rank.astype(jnp.int32), -1)


def gather_axis(half, axis):
    rows = half.shape[0] // 2
    ahead = shift(half, axis, 1)
    behind = shift(half, axis, -1)
    low = shift(ahead[:rows], axis, 1)
    high = shift(behind[rows:], axis, -1)
    return (half, ahead, low, high, behind)


def pack_kernel(first, slot_ref, own, ahead, low, high, behind, *outs):
    tokens = own.shape[0]
    sources = (own[...], ahead[...], jnp.concatenate([low[...], high[...]], axis=0), behind[...])
    place = lax.broadcasted_iota(jnp.int32, (ROWS, tokens), 0) + first
    for source in range(SIDE):
        picks = [
            (slot_ref[source, dest : dest + 1, :] == place).astype(jnp.float32)
            for dest in range(SIDE)
        ]
        pick = jnp.concatenate(picks, axis=0).astype(jnp.bfloat16)
        rows = jnp.dot(pick, sources[source], preferred_element_type=jnp.float32)
        rows = rows.astype(jnp.bfloat16)
        for dest in range(SIDE):
            outs[dest][source] = rows[dest * ROWS : (dest + 1) * ROWS]


def pack(chunk, slots, blocks):
    tokens, width = blocks[0].shape
    tile = min(PACK_TILE, width)
    whole = pl.BlockSpec((SIDE, SIDE, tokens), lambda i: (0, 0, 0))
    specs = [pl.BlockSpec((b.shape[0], tile), lambda i: (0, i)) for b in blocks]
    out = jax.ShapeDtypeStruct((SIDE, ROWS, width), jnp.bfloat16)
    return pl.pallas_call(
        functools.partial(pack_kernel, chunk * ROWS),
        grid=(width // tile,),
        in_specs=[whole] + specs,
        out_specs=[pl.BlockSpec((SIDE, ROWS, tile), lambda i: (0, 0, i))] * SIDE,
        out_shape=[out] * SIDE,
        compiler_params=pltpu.CompilerParams(vmem_limit_bytes=VMEM),
        cost_estimate=pl.CostEstimate(
            flops=2 * SIDE * SIDE * ROWS * tokens * width,
            bytes_accessed=2 * SIDE * width * (tokens + SIDE * ROWS),
            transcendentals=0,
        ),
    )(slots, *blocks)


def expert_kernel(n_ff, n_half, scale_ref, wg_ref, wu_ref, wd_ref, *refs):
    a_in, b_in = refs[:SIDE], refs[SIDE : 2 * SIDE]
    a_out, b_out = refs[2 * SIDE : 3 * SIDE], refs[3 * SIDE : 4 * SIDE]
    x_ref, hidden_ref, sems = refs[4 * SIDE :]
    step = pl.program_id(0)
    half = x_ref.shape[-1] // 2
    count = SIDE * SIDE * ROWS

    @pl.when(step == 0)
    def _():
        copies = []
        for k in range(SIDE):
            copies.append(
                pltpu.make_async_copy(a_in[k], x_ref.at[:, k, :, :half], sems.at[k])
            )
            copies.append(
                pltpu.make_async_copy(b_in[k], x_ref.at[k, :, :, half:], sems.at[SIDE + k])
            )
        for copy in copies:
            copy.start()
        for copy in copies:
            copy.wait()

    for f in range(n_ff):

        @pl.when(step == f)
        def _(f=f):
            x = x_ref[...].reshape(count, 2 * half)
            gate = jnp.dot(x, wg_ref[...], preferred_element_type=jnp.float32)
            up = jnp.dot(x, wu_ref[...], preferred_element_type=jnp.float32)
            tile = gate.shape[1]
            hidden = gate / (1.0 + jnp.exp(-gate)) * up
            hidden_ref[:, f * tile : (f + 1) * tile] = hidden.astype(jnp.bfloat16)

    def down():
        out = jnp.dot(hidden_ref[...], wd_ref[...], preferred_element_type=jnp.float32)
        out = (out * scale_ref[...]).astype(jnp.bfloat16)
        return out.reshape(SIDE, SIDE, ROWS, out.shape[1])

    @pl.when((step >= n_ff) & (step < n_ff + n_half))
    def _():
        out = down()
        for k in range(SIDE):
            a_out[k][...] = out[:, k]

    @pl.when(step >= n_ff + n_half)
    def _():
        out = down()
        for k in range(SIDE):
            b_out[k][...] = out[k]


def expert(scale, w_gate, w_up, w_down, a_in, b_in):
    half = a_in[0].shape[-1]
    depth, ff = w_gate.shape
    count = SIDE * SIDE * ROWS
    n_ff = ff // FF_TILE
    d_tile = min(D_TILE, half)
    n_half = half // d_tile
    ff_spec = pl.BlockSpec((depth, FF_TILE), lambda i: (0, jnp.minimum(i, n_ff - 1)))
    wd_spec = pl.BlockSpec((ff, d_tile), lambda i: (0, jnp.maximum(i - n_ff, 0)))
    a_spec = pl.BlockSpec(
        (SIDE, ROWS, d_tile), lambda i: (0, 0, jnp.clip(i - n_ff, 0, n_half - 1))
    )
    b_spec = pl.BlockSpec(
        (SIDE, ROWS, d_tile), lambda i: (0, 0, jnp.clip(i - n_ff - n_half, 0, n_half - 1))
    )
    out = jax.ShapeDtypeStruct((SIDE, ROWS, half), jnp.bfloat16)
    done = pl.pallas_call(
        functools.partial(expert_kernel, n_ff, n_half),
        grid=(n_ff + 2 * n_half,),
        in_specs=[pl.BlockSpec((count, 1), lambda i: (0, 0)), ff_spec, ff_spec, wd_spec]
        + [pl.BlockSpec(memory_space=pl.ANY)] * (2 * SIDE),
        out_specs=[a_spec] * SIDE + [b_spec] * SIDE,
        out_shape=[out] * (2 * SIDE),
        scratch_shapes=[
            pltpu.VMEM((SIDE, SIDE, ROWS, depth), jnp.bfloat16),
            pltpu.VMEM((count, ff), jnp.bfloat16),
            pltpu.SemaphoreType.DMA((2 * SIDE,)),
        ],
        compiler_params=pltpu.CompilerParams(vmem_limit_bytes=VMEM),
        cost_estimate=pl.CostEstimate(
            flops=6 * count * depth * ff,
            bytes_accessed=6 * depth * ff + 4 * count * depth,
            transcendentals=count * ff,
        ),
    )(scale, w_gate, w_up, w_down, *a_in, *b_in)
    return done[:SIDE], done[SIDE:]


def sum_kernel(slot_ref, *refs):
    ins, outs = refs[: CHUNKS * SIDE], refs[CHUNKS * SIDE :]
    tokens = slot_ref.shape[-1]
    place = lax.broadcasted_iota(jnp.int32, (ROWS, tokens), 0)
    for source in range(SIDE):
        picks, rows = [], []
        for chunk in range(CHUNKS):
            for dest in range(SIDE):
                hit = slot_ref[source, dest : dest + 1, :] == place + chunk * ROWS
                picks.append(hit.astype(jnp.float32))
                rows.append(ins[chunk * SIDE + dest][source])
        pick = jnp.concatenate(picks, axis=0).T.astype(jnp.bfloat16)
        total = jnp.dot(
            pick, jnp.concatenate(rows, axis=0), preferred_element_type=jnp.float32
        )
        outs[source][...] = total.astype(jnp.bfloat16)


def sum_rows(slots, blocks):
    width = blocks[0].shape[-1]
    tokens = slots.shape[-1]
    tile = min(SUM_TILE, width)
    out = jax.ShapeDtypeStruct((tokens, width), jnp.bfloat16)
    return pl.pallas_call(
        sum_kernel,
        grid=(width // tile,),
        in_specs=[pl.BlockSpec((SIDE, SIDE, tokens), lambda i: (0, 0, 0))]
        + [pl.BlockSpec((SIDE, ROWS, tile), lambda i: (0, 0, i))] * len(blocks),
        out_specs=[pl.BlockSpec((tokens, tile), lambda i: (0, i))] * SIDE,
        out_shape=[out] * SIDE,
        compiler_params=pltpu.CompilerParams(vmem_limit_bytes=VMEM),
        cost_estimate=pl.CostEstimate(
            flops=2 * SIDE * SIDE * CAP * tokens * width,
            bytes_accessed=2 * SIDE * width * (tokens + SIDE * CAP),
            transcendentals=0,
        ),
    )(slots, *blocks)


def local(tokens, expert_ids, gate_values, gate_weight, up_weight, down_weight):
    half = tokens.shape[1] // 2
    z, x = lax.axis_index("z"), lax.axis_index("x")
    steps = jnp.arange(SIDE)

    a_rows = gather_axis(tokens[:, :half], "z")
    b_rows = gather_axis(tokens[:, half:], "x")

    top = expert_ids.shape[1]
    routing = jnp.concatenate([expert_ids.T.astype(jnp.float32), gate_values.T], axis=0)
    routing = lax.all_gather(routing, ("z", "x"), axis=0, tiled=False)
    routing = routing.reshape((SIDE, SIDE) + routing.shape[1:])
    routing = routing[(z - steps) % SIDE][:, (x - steps) % SIDE]
    ids, gates = routing[:, :, :top].astype(jnp.int32), routing[:, :, top:]

    a_slots = slots_of(
        jnp.broadcast_to(ids[:, :1], ids.shape),
        jnp.broadcast_to(z * SIDE + (x + steps) % SIDE, (SIDE, SIDE)),
    )
    b_slots = slots_of(
        jnp.broadcast_to(ids[0][:, None], ids.shape),
        jnp.broadcast_to((z + steps) % SIDE * SIDE + x, (SIDE, SIDE)),
    )
    here = jnp.full((SIDE, SIDE), z * SIDE + x)
    slots = slots_of(ids, here)
    weight = jnp.sum(jnp.where(ids == here[..., None, None], gates, 0.0), axis=2)
    hit = slots[:, :, None, :] == jnp.arange(CAP)[:, None]
    scale = jnp.sum(jnp.where(hit, weight[:, :, None, :], 0.0), axis=-1)

    w_gate, w_up, w_down = gate_weight[0], up_weight[0], down_weight[0]
    a_back, b_back = [], []
    for chunk in range(CHUNKS):
        a_out = pack(chunk, a_slots, a_rows)
        b_out = pack(chunk, b_slots, b_rows)
        a_in = [a_out[0]] + [shift(a_out[k], "x", k) for k in range(1, SIDE)]
        b_in = [b_out[0]] + [shift(b_out[k], "z", k) for k in range(1, SIDE)]
        part = scale[:, :, chunk * ROWS : (chunk + 1) * ROWS].reshape(-1, 1)
        a_done, b_done = expert(part, w_gate, w_up, w_down, a_in, b_in)
        a_back += [a_done[0]] + [shift(a_done[k], "x", -k) for k in range(1, SIDE)]
        b_back += [b_done[0]] + [shift(b_done[k], "z", -k) for k in range(1, SIDE)]

    a_sums = sum_rows(a_slots, a_back)
    b_sums = sum_rows(b_slots, b_back)
    a_home = [a_sums[0]] + [shift(a_sums[k], "z", -k) for k in range(1, SIDE)]
    b_home = [b_sums[0]] + [shift(b_sums[k], "x", -k) for k in range(1, SIDE)]
    mixed = [sum(part.astype(jnp.float32) for part in home) for home in (a_home, b_home)]
    return jnp.concatenate(mixed, axis=1).astype(jnp.bfloat16)


def solution(mesh):
    dp = mesh.devices.shape[0]
    grid = Mesh(mesh.devices.reshape(dp, SIDE, SIDE), ("dp", "z", "x"))
    rows, experts = ("dp", "z", "x"), ("z", "x")
    in_specs = (
        P(rows, None),
        P(rows, None),
        P(rows, None),
        P(experts, None, None),
        P(experts, None, None),
        P(experts, None, None),
    )
    return jax.shard_map(
        local, mesh=grid, in_specs=in_specs, out_specs=P(rows, None), check_vma=False
    )
```

```python
import functools

import jax
import jax.numpy as jnp
from jax import lax
from jax.experimental import pallas as pl
from jax.experimental.pallas import tpu as pltpu
from jax.sharding import Mesh, PartitionSpec as P

SIDE = 4
CAP = 64
CHUNKS = 2
ROWS = CAP // CHUNKS
PACK_TILE = 512
FF_TILE = 256
D_TILE = 512
SUM_TILE = 512
VMEM = 36 * 1024 * 1024
TILE = 128


def shift(block, axis, step):
    return lax.ppermute(block, axis, [(i, (i + step) % SIDE) for i in range(SIDE)])


def prepare_kernel(token_ref, id_ref, gate_ref, a_ref, b_ref):
    tokens, depth = token_ref.shape
    half = depth // 2
    top = id_ref.shape[1]
    lane = lax.broadcasted_iota(jnp.int32, (tokens, TILE), 1)
    row = lax.broadcasted_iota(jnp.int32, (tokens, tokens), 0)
    column = lax.broadcasted_iota(jnp.int32, (tokens, tokens), 1)
    ids = [id_ref[:, k : k + 1] for k in range(top)]
    named = jnp.zeros((tokens, TILE), jnp.float32)
    for k in range(top):
        named = named + (ids[k] == lane).astype(jnp.float32)
    before = (column < row).astype(jnp.float32).astype(jnp.bfloat16)
    rank = jnp.dot(before, named.astype(jnp.bfloat16), preferred_element_type=jnp.float32)
    facts = jnp.zeros((tokens, TILE), jnp.float32)
    for k in range(top):
        place = jnp.sum(jnp.where(ids[k] == lane, rank, 0.0), axis=1, keepdims=True)
        facts = jnp.where(lane == k, ids[k].astype(jnp.float32), facts)
        facts = jnp.where(lane == top + k, place, facts)
        rest = gate_ref[:, k : k + 1]
        for part in range(2, 5):
            term = rest.astype(jnp.bfloat16).astype(jnp.float32)
            facts = jnp.where(lane == part * top + k, term, facts)
            rest = rest - term
    facts = facts.astype(jnp.bfloat16)
    a_ref[:, :half] = token_ref[:, :half]
    b_ref[:, :half] = token_ref[:, half:]
    a_ref[:, half:] = facts
    b_ref[:, half:] = facts


def prepare(tokens, expert_ids, gate_values):
    rows, depth = tokens.shape
    out = jax.ShapeDtypeStruct((rows, depth // 2 + TILE), jnp.bfloat16)
    return pl.pallas_call(
        prepare_kernel,
        out_shape=[out, out],
        compiler_params=pltpu.CompilerParams(vmem_limit_bytes=VMEM),
        cost_estimate=pl.CostEstimate(
            flops=2 * rows * rows * TILE, bytes_accessed=4 * rows * depth, transcendentals=0
        ),
    )(tokens, expert_ids, gate_values)


def codes(facts, top):
    facts = facts.astype(jnp.float32)
    return [facts[:, k : k + 1] * CAP + facts[:, top + k : top + k + 1] for k in range(top)]


def targets(experts_ref, chunks, tokens):
    count = len(chunks) * SIDE * ROWS
    lane = lax.broadcasted_iota(jnp.int32, (tokens, count), 1)
    code = jnp.zeros((tokens, count), jnp.int32)
    for n, chunk in enumerate(chunks):
        for dest in range(SIDE):
            low = (n * SIDE + dest) * ROWS
            value = experts_ref[dest] * CAP + chunk * ROWS + lane - low
            code = jnp.where((lane >= low) & (lane < low + ROWS), value, code)
    return code.astype(jnp.float32)


def pack_kernel(chunk, top, experts_ref, *refs):
    sources, facts, outs = refs[:SIDE], refs[SIDE : 2 * SIDE], refs[2 * SIDE :]
    tokens = sources[0].shape[0]
    target = targets(experts_ref, (chunk,), tokens)
    for source in range(SIDE):
        pick = jnp.zeros(target.shape, jnp.float32)
        for code in codes(facts[source][...], top):
            pick = jnp.where(code == target, 1.0, pick)
        rows = jnp.dot(
            pick.T.astype(jnp.bfloat16), sources[source][...], preferred_element_type=jnp.float32
        ).astype(jnp.bfloat16)
        for dest in range(SIDE):
            outs[dest][source] = rows[dest * ROWS : (dest + 1) * ROWS]


def pack(chunk, top, experts, blocks):
    tokens, width = blocks[0].shape
    width -= TILE
    tile = min(PACK_TILE, width)
    last = width // TILE
    out = jax.ShapeDtypeStruct((SIDE, ROWS, width), jnp.bfloat16)
    return pl.pallas_call(
        functools.partial(pack_kernel, chunk, top),
        grid=(width // tile,),
        in_specs=[pl.BlockSpec(memory_space=pltpu.SMEM)]
        + [pl.BlockSpec((tokens, tile), lambda i: (0, i))] * SIDE
        + [pl.BlockSpec((tokens, TILE), lambda i: (0, last))] * SIDE,
        out_specs=[pl.BlockSpec((SIDE, ROWS, tile), lambda i: (0, 0, i))] * SIDE,
        out_shape=[out] * SIDE,
        compiler_params=pltpu.CompilerParams(vmem_limit_bytes=VMEM),
        cost_estimate=pl.CostEstimate(
            flops=2 * SIDE * SIDE * ROWS * tokens * width,
            bytes_accessed=2 * SIDE * width * (tokens + SIDE * ROWS),
            transcendentals=0,
        ),
    )(experts, *blocks, *blocks)


def expert_kernel(n_ff, n_half, wg_ref, wu_ref, wd_ref, *refs):
    a_in, b_in = refs[:SIDE], refs[SIDE : 2 * SIDE]
    a_out, b_out = refs[2 * SIDE : 3 * SIDE], refs[3 * SIDE : 4 * SIDE]
    x_ref, hidden_ref, sems = refs[4 * SIDE :]
    step = pl.program_id(0)
    half = x_ref.shape[-1] // 2
    count = SIDE * SIDE * ROWS

    @pl.when(step == 0)
    def _():
        copies = []
        for k in range(SIDE):
            copies.append(
                pltpu.make_async_copy(a_in[k], x_ref.at[:, k, :, :half], sems.at[k])
            )
            copies.append(
                pltpu.make_async_copy(b_in[k], x_ref.at[k, :, :, half:], sems.at[SIDE + k])
            )
        for copy in copies:
            copy.start()
        for copy in copies:
            copy.wait()

    for f in range(n_ff):

        @pl.when(step == f)
        def _(f=f):
            x = x_ref[...].reshape(count, 2 * half)
            gate = jnp.dot(x, wg_ref[...], preferred_element_type=jnp.float32)
            up = jnp.dot(x, wu_ref[...], preferred_element_type=jnp.float32)
            tile = gate.shape[1]
            hidden = gate / (1.0 + jnp.exp(-gate)) * up
            hidden_ref[:, f * tile : (f + 1) * tile] = hidden.astype(jnp.bfloat16)

    def down():
        out = jnp.dot(hidden_ref[...], wd_ref[...], preferred_element_type=jnp.float32)
        return out.astype(jnp.bfloat16).reshape(SIDE, SIDE, ROWS, out.shape[1])

    @pl.when((step >= n_ff) & (step < n_ff + n_half))
    def _():
        out = down()
        for k in range(SIDE):
            a_out[k][...] = out[:, k]

    @pl.when(step >= n_ff + n_half)
    def _():
        out = down()
        for k in range(SIDE):
            b_out[k][...] = out[k]


def expert(w_gate, w_up, w_down, a_in, b_in):
    half = a_in[0].shape[-1]
    depth, ff = w_gate.shape
    count = SIDE * SIDE * ROWS
    n_ff = ff // FF_TILE
    d_tile = min(D_TILE, half)
    n_half = half // d_tile
    ff_spec = pl.BlockSpec((depth, FF_TILE), lambda i: (0, jnp.minimum(i, n_ff - 1)))
    wd_spec = pl.BlockSpec((ff, d_tile), lambda i: (0, jnp.maximum(i - n_ff, 0)))
    a_spec = pl.BlockSpec(
        (SIDE, ROWS, d_tile), lambda i: (0, 0, jnp.clip(i - n_ff, 0, n_half - 1))
    )
    b_spec = pl.BlockSpec(
        (SIDE, ROWS, d_tile), lambda i: (0, 0, jnp.clip(i - n_ff - n_half, 0, n_half - 1))
    )
    out = jax.ShapeDtypeStruct((SIDE, ROWS, half), jnp.bfloat16)
    done = pl.pallas_call(
        functools.partial(expert_kernel, n_ff, n_half),
        grid=(n_ff + 2 * n_half,),
        in_specs=[ff_spec, ff_spec, wd_spec]
        + [pl.BlockSpec(memory_space=pl.ANY)] * (2 * SIDE),
        out_specs=[a_spec] * SIDE + [b_spec] * SIDE,
        out_shape=[out] * (2 * SIDE),
        scratch_shapes=[
            pltpu.VMEM((SIDE, SIDE, ROWS, depth), jnp.bfloat16),
            pltpu.VMEM((count, ff), jnp.bfloat16),
            pltpu.SemaphoreType.DMA((2 * SIDE,)),
        ],
        compiler_params=pltpu.CompilerParams(vmem_limit_bytes=VMEM),
        cost_estimate=pl.CostEstimate(
            flops=6 * count * depth * ff,
            bytes_accessed=6 * depth * ff + 4 * count * depth,
            transcendentals=count * ff,
        ),
    )(w_gate, w_up, w_down, *a_in, *b_in)
    return done[:SIDE], done[SIDE:]


def sum_kernel(top, experts_ref, *refs):
    count = CHUNKS * SIDE
    ins, facts, outs = refs[:count], refs[count : count + SIDE], refs[count + SIDE :]
    tokens = outs[0].shape[0]
    target = targets(experts_ref, tuple(range(CHUNKS)), tokens)
    for source in range(SIDE):
        about = facts[source][...]
        wide = about.astype(jnp.float32)
        weight = jnp.zeros(target.shape, jnp.float32)
        for k, code in enumerate(codes(about, top)):
            first, second, third = (
                wide[:, part * top + k : part * top + k + 1] for part in range(2, 5)
            )
            weight = jnp.where(code == target, first + second + third, weight)
        high = weight.astype(jnp.bfloat16)
        low = (weight - high.astype(jnp.float32)).astype(jnp.bfloat16)
        rows = jnp.concatenate([ref[source] for ref in ins], axis=0)
        total = jnp.dot(high, rows, preferred_element_type=jnp.float32)
        total = total + jnp.dot(low, rows, preferred_element_type=jnp.float32)
        outs[source][...] = total.astype(jnp.bfloat16)


def sum_rows(top, experts, facts, blocks):
    width = blocks[0].shape[-1]
    tokens = facts[0].shape[0]
    tile = min(SUM_TILE, width)
    last = width // TILE
    out = jax.ShapeDtypeStruct((tokens, width), jnp.bfloat16)
    return pl.pallas_call(
        functools.partial(sum_kernel, top),
        grid=(width // tile,),
        in_specs=[pl.BlockSpec(memory_space=pltpu.SMEM)]
        + [pl.BlockSpec((SIDE, ROWS, tile), lambda i: (0, 0, i))] * len(blocks)
        + [pl.BlockSpec((tokens, TILE), lambda i: (0, last))] * SIDE,
        out_specs=[pl.BlockSpec((tokens, tile), lambda i: (0, i))] * SIDE,
        out_shape=[out] * SIDE,
        compiler_params=pltpu.CompilerParams(vmem_limit_bytes=VMEM),
        cost_estimate=pl.CostEstimate(
            flops=4 * SIDE * SIDE * CAP * tokens * width,
            bytes_accessed=2 * SIDE * width * (tokens + SIDE * CAP),
            transcendentals=0,
        ),
    )(experts, *blocks, *facts)


def local(tokens, expert_ids, gate_values, gate_weight, up_weight, down_weight):
    top = expert_ids.shape[1]
    z, x = lax.axis_index("z"), lax.axis_index("x")
    steps = jnp.arange(SIDE, dtype=jnp.int32)
    a_experts = z * SIDE + (x + steps) % SIDE
    b_experts = (z + steps) % SIDE * SIDE + x

    a_half, b_half = prepare(tokens, expert_ids, gate_values)
    a_rows = [a_half] + [shift(a_half, "z", k) for k in range(1, SIDE)]
    b_rows = [b_half] + [shift(b_half, "x", k) for k in range(1, SIDE)]

    w_gate, w_up, w_down = gate_weight[0], up_weight[0], down_weight[0]
    a_back, b_back = [], []
    for chunk in range(CHUNKS):
        a_out = pack(chunk, top, a_experts, a_rows)
        b_out = pack(chunk, top, b_experts, b_rows)
        a_experts, b_experts, a_out, b_out = lax.optimization_barrier(
            (a_experts, b_experts, a_out, b_out)
        )
        a_in = [a_out[0]] + [shift(a_out[k], "x", k) for k in range(1, SIDE)]
        b_in = [b_out[0]] + [shift(b_out[k], "z", k) for k in range(1, SIDE)]
        a_done, b_done = expert(w_gate, w_up, w_down, a_in, b_in)
        a_back += [a_done[0]] + [shift(a_done[k], "x", -k) for k in range(1, SIDE)]
        b_back += [b_done[0]] + [shift(b_done[k], "z", -k) for k in range(1, SIDE)]

    a_sums = sum_rows(top, a_experts, a_rows, a_back)
    b_sums = sum_rows(top, b_experts, b_rows, b_back)
    a_home = [a_sums[0]] + [shift(a_sums[k], "z", -k) for k in range(1, SIDE)]
    b_home = [b_sums[0]] + [shift(b_sums[k], "x", -k) for k in range(1, SIDE)]
    mixed = [sum(part.astype(jnp.float32) for part in home) for home in (a_home, b_home)]
    return jnp.concatenate(mixed, axis=1).astype(jnp.bfloat16)


def solution(mesh):
    dp = mesh.devices.shape[0]
    grid = Mesh(mesh.devices.reshape(dp, SIDE, SIDE), ("dp", "z", "x"))
    rows, experts = ("dp", "z", "x"), ("z", "x")
    in_specs = (
        P(rows, None),
        P(rows, None),
        P(rows, None),
        P(experts, None, None),
        P(experts, None, None),
        P(experts, None, None),
    )
    return jax.shard_map(
        local, mesh=grid, in_specs=in_specs, out_specs=P(rows, None), check_vma=False
    )
```

```python
import functools

import jax
import jax.numpy as jnp
from jax import lax
from jax.experimental import pallas as pl
from jax.experimental.pallas import tpu as pltpu
from jax.sharding import Mesh, PartitionSpec as P

SIDE = 4
CAP = 64
CHUNKS = 2
ROWS = CAP // CHUNKS
TILE = 128
PACK_TILE = 512
FF_TILE = 256
D_TILE = 1024
SUM_TILE = 512
VMEM = 36 * 1024 * 1024


def shift(block, axis, step):
    return lax.ppermute(block, axis, [(i, (i + step) % SIDE) for i in range(SIDE)])


def prepare_kernel(token_ref, id_ref, gate_ref, a_ref, b_ref):
    tokens, depth = token_ref.shape
    half = depth // 2
    top = id_ref.shape[0]
    given = jnp.concatenate([id_ref[...].astype(jnp.float32), gate_ref[...]], axis=0).T
    lane = lax.broadcasted_iota(jnp.int32, (tokens, TILE), 1)
    number = lane.astype(jnp.float32)
    row = lax.broadcasted_iota(jnp.int32, (tokens, tokens), 0)
    column = lax.broadcasted_iota(jnp.int32, (tokens, tokens), 1)
    ids = [given[:, k : k + 1] for k in range(top)]
    named = jnp.zeros((tokens, TILE), jnp.float32)
    for k in range(top):
        named = jnp.where(ids[k] == number, 1.0, named)
    before = jnp.where(column < row, 1.0, 0.0).astype(jnp.bfloat16)
    rank = jnp.dot(before, named.astype(jnp.bfloat16), preferred_element_type=jnp.float32)
    facts = jnp.zeros((tokens, TILE), jnp.float32)
    for k in range(top):
        place = jnp.sum(jnp.where(ids[k] == number, rank, 0.0), axis=1, keepdims=True)
        facts = jnp.where(lane == k, ids[k], facts)
        facts = jnp.where(lane == top + k, place, facts)
        rest = given[:, top + k : top + k + 1]
        for part in range(2, 5):
            term = rest.astype(jnp.bfloat16).astype(jnp.float32)
            facts = jnp.where(lane == part * top + k, term, facts)
            rest = rest - term
    facts = facts.astype(jnp.bfloat16)
    a_ref[:, :half] = token_ref[:, :half]
    b_ref[:, :half] = token_ref[:, half:]
    a_ref[:, half:] = facts
    b_ref[:, half:] = facts


def prepare(tokens, expert_ids, gate_values):
    rows, depth = tokens.shape
    out = jax.ShapeDtypeStruct((rows, depth // 2 + TILE), jnp.bfloat16)
    return pl.pallas_call(
        prepare_kernel,
        out_shape=[out, out],
        compiler_params=pltpu.CompilerParams(vmem_limit_bytes=VMEM),
        cost_estimate=pl.CostEstimate(
            flops=2 * rows * rows * TILE, bytes_accessed=4 * rows * depth, transcendentals=0
        ),
    )(tokens, expert_ids.T, gate_values.T)


def codes(facts, top):
    facts = facts.astype(jnp.float32)
    return [facts[:, k : k + 1] * CAP + facts[:, top + k : top + k + 1] for k in range(top)]


def targets(experts_ref, chunks, tokens):
    count = len(chunks) * SIDE * ROWS
    lane = lax.broadcasted_iota(jnp.int32, (tokens, count), 1)
    code = jnp.zeros((tokens, count), jnp.int32)
    for n, chunk in enumerate(chunks):
        for dest in range(SIDE):
            low = (n * SIDE + dest) * ROWS
            value = experts_ref[dest] * CAP + chunk * ROWS + lane - low
            code = jnp.where((lane >= low) & (lane < low + ROWS), value, code)
    return code.astype(jnp.float32)


def pack_kernel(chunk, top, experts_ref, *refs):
    sources, facts = refs[:SIDE], refs[SIDE : 2 * SIDE]
    outs, pick_ref = refs[2 * SIDE : -1], refs[-1]
    tokens = sources[0].shape[0]

    @pl.when(pl.program_id(0) == 0)
    def _():
        target = targets(experts_ref, (chunk,), tokens)
        for source in range(SIDE):
            pick = jnp.zeros(target.shape, jnp.float32)
            for code in codes(facts[source][...], top):
                pick = jnp.where(code == target, 1.0, pick)
            pick_ref[source] = pick.T.astype(jnp.bfloat16)

    for source in range(SIDE):
        rows = jnp.dot(
            pick_ref[source], sources[source][...], preferred_element_type=jnp.float32
        ).astype(jnp.bfloat16)
        for dest in range(SIDE):
            outs[dest][source] = rows[dest * ROWS : (dest + 1) * ROWS]


def pack(chunk, top, experts, blocks):
    tokens, width = blocks[0].shape
    width -= TILE
    tile = min(PACK_TILE, width)
    last = width // TILE
    out = jax.ShapeDtypeStruct((SIDE, ROWS, width), jnp.bfloat16)
    return pl.pallas_call(
        functools.partial(pack_kernel, chunk, top),
        grid=(width // tile,),
        in_specs=[pl.BlockSpec(memory_space=pltpu.SMEM)]
        + [pl.BlockSpec((tokens, tile), lambda i: (0, i))] * SIDE
        + [pl.BlockSpec((tokens, TILE), lambda i: (0, last))] * SIDE,
        out_specs=[pl.BlockSpec((SIDE, ROWS, tile), lambda i: (0, 0, i))] * SIDE,
        out_shape=[out] * SIDE,
        scratch_shapes=[pltpu.VMEM((SIDE, SIDE * ROWS, tokens), jnp.bfloat16)],
        compiler_params=pltpu.CompilerParams(vmem_limit_bytes=VMEM),
        cost_estimate=pl.CostEstimate(
            flops=2 * SIDE * SIDE * ROWS * tokens * width,
            bytes_accessed=2 * SIDE * width * (tokens + SIDE * ROWS),
            transcendentals=0,
        ),
    )(experts, *blocks, *blocks)


def expert_kernel(n_ff, n_half, wg_ref, wu_ref, wd_ref, *refs):
    a_in, b_in = refs[:SIDE], refs[SIDE : 2 * SIDE]
    a_out, b_out = refs[2 * SIDE : 3 * SIDE], refs[3 * SIDE : 4 * SIDE]
    x_ref, hidden_ref, sems = refs[4 * SIDE :]
    step = pl.program_id(0)
    half = x_ref.shape[-1] // 2
    count = SIDE * SIDE * ROWS

    @pl.when(step == 0)
    def _():
        copies = []
        for k in range(SIDE):
            copies.append(
                pltpu.make_async_copy(a_in[k], x_ref.at[:, k, :, :half], sems.at[k])
            )
            copies.append(
                pltpu.make_async_copy(b_in[k], x_ref.at[k, :, :, half:], sems.at[SIDE + k])
            )
        for copy in copies:
            copy.start()
        for copy in copies:
            copy.wait()

    for f in range(n_ff):

        @pl.when(step == f)
        def _(f=f):
            x = x_ref[...].reshape(count, 2 * half)
            gate = jnp.dot(x, wg_ref[...], preferred_element_type=jnp.float32)
            up = jnp.dot(x, wu_ref[...], preferred_element_type=jnp.float32)
            tile = gate.shape[1]
            hidden = gate / (1.0 + jnp.exp(-gate)) * up
            hidden_ref[:, f * tile : (f + 1) * tile] = hidden.astype(jnp.bfloat16)

    def down():
        out = jnp.dot(hidden_ref[...], wd_ref[...], preferred_element_type=jnp.float32)
        return out.astype(jnp.bfloat16).reshape(SIDE, SIDE, ROWS, out.shape[1])

    @pl.when((step >= n_ff) & (step < n_ff + n_half))
    def _():
        out = down()
        for k in range(SIDE):
            a_out[k][...] = out[:, k]

    @pl.when(step >= n_ff + n_half)
    def _():
        out = down()
        for k in range(SIDE):
            b_out[k][...] = out[k]


def expert(w_gate, w_up, w_down, a_in, b_in):
    half = a_in[0].shape[-1]
    depth, ff = w_gate.shape
    count = SIDE * SIDE * ROWS
    n_ff = ff // FF_TILE
    d_tile = min(D_TILE, half)
    n_half = half // d_tile
    ff_spec = pl.BlockSpec((depth, FF_TILE), lambda i: (0, jnp.minimum(i, n_ff - 1)))
    wd_spec = pl.BlockSpec((ff, d_tile), lambda i: (0, jnp.maximum(i - n_ff, 0)))
    a_spec = pl.BlockSpec(
        (SIDE, ROWS, d_tile), lambda i: (0, 0, jnp.clip(i - n_ff, 0, n_half - 1))
    )
    b_spec = pl.BlockSpec(
        (SIDE, ROWS, d_tile), lambda i: (0, 0, jnp.clip(i - n_ff - n_half, 0, n_half - 1))
    )
    out = jax.ShapeDtypeStruct((SIDE, ROWS, half), jnp.bfloat16)
    done = pl.pallas_call(
        functools.partial(expert_kernel, n_ff, n_half),
        grid=(n_ff + 2 * n_half,),
        in_specs=[ff_spec, ff_spec, wd_spec]
        + [pl.BlockSpec(memory_space=pl.ANY)] * (2 * SIDE),
        out_specs=[a_spec] * SIDE + [b_spec] * SIDE,
        out_shape=[out] * (2 * SIDE),
        scratch_shapes=[
            pltpu.VMEM((SIDE, SIDE, ROWS, depth), jnp.bfloat16),
            pltpu.VMEM((count, ff), jnp.bfloat16),
            pltpu.SemaphoreType.DMA((2 * SIDE,)),
        ],
        compiler_params=pltpu.CompilerParams(vmem_limit_bytes=VMEM),
        cost_estimate=pl.CostEstimate(
            flops=6 * count * depth * ff,
            bytes_accessed=6 * depth * ff + 4 * count * depth,
            transcendentals=count * ff,
        ),
    )(w_gate, w_up, w_down, *a_in, *b_in)
    return done[:SIDE], done[SIDE:]


def sum_kernel(top, experts_ref, *refs):
    count = CHUNKS * SIDE
    ins, facts = refs[:count], refs[count : count + SIDE]
    outs, high_ref, low_ref = refs[count + SIDE : -2], refs[-2], refs[-1]
    tokens = high_ref.shape[1]

    @pl.when(pl.program_id(0) == 0)
    def _():
        target = targets(experts_ref, tuple(range(CHUNKS)), tokens)
        for source in range(SIDE):
            about = facts[source][...]
            wide = about.astype(jnp.float32)
            weight = jnp.zeros(target.shape, jnp.float32)
            for k, code in enumerate(codes(about, top)):
                first, second, third = (
                    wide[:, part * top + k : part * top + k + 1] for part in range(2, 5)
                )
                weight = jnp.where(code == target, first + second + third, weight)
            high = weight.astype(jnp.bfloat16)
            high_ref[source] = high
            low_ref[source] = (weight - high.astype(jnp.float32)).astype(jnp.bfloat16)

    for source in range(SIDE):
        rows = jnp.concatenate([ref[source] for ref in ins], axis=0)
        total = jnp.dot(high_ref[source], rows, preferred_element_type=jnp.float32)
        total = total + jnp.dot(low_ref[source], rows, preferred_element_type=jnp.float32)
        outs[source][...] = total.astype(jnp.bfloat16)


def sum_rows(top, experts, facts, blocks):
    width = blocks[0].shape[-1]
    tokens = facts[0].shape[0]
    tile = min(SUM_TILE, width)
    last = width // TILE
    out = jax.ShapeDtypeStruct((tokens, width), jnp.bfloat16)
    weights = pltpu.VMEM((SIDE, tokens, SIDE * CAP), jnp.bfloat16)
    return pl.pallas_call(
        functools.partial(sum_kernel, top),
        grid=(width // tile,),
        in_specs=[pl.BlockSpec(memory_space=pltpu.SMEM)]
        + [pl.BlockSpec((SIDE, ROWS, tile), lambda i: (0, 0, i))] * len(blocks)
        + [pl.BlockSpec((tokens, TILE), lambda i: (0, last))] * SIDE,
        out_specs=[pl.BlockSpec((tokens, tile), lambda i: (0, i))] * SIDE,
        out_shape=[out] * SIDE,
        scratch_shapes=[weights, weights],
        compiler_params=pltpu.CompilerParams(vmem_limit_bytes=VMEM),
        cost_estimate=pl.CostEstimate(
            flops=4 * SIDE * SIDE * CAP * tokens * width,
            bytes_accessed=2 * SIDE * width * (tokens + SIDE * CAP),
            transcendentals=0,
        ),
    )(experts, *blocks, *facts)


def local(tokens, expert_ids, gate_values, gate_weight, up_weight, down_weight):
    top = expert_ids.shape[1]
    z, x = lax.axis_index("z"), lax.axis_index("x")
    steps = jnp.arange(SIDE, dtype=jnp.int32)
    a_experts = z * SIDE + (x + steps) % SIDE
    b_experts = (z + steps) % SIDE * SIDE + x

    a_half, b_half = prepare(tokens, expert_ids, gate_values)
    a_rows = [a_half] + [shift(a_half, "z", k) for k in range(1, SIDE)]
    b_rows = [b_half] + [shift(b_half, "x", k) for k in range(1, SIDE)]

    w_gate, w_up, w_down = gate_weight[0], up_weight[0], down_weight[0]
    a_back, b_back = [], []
    a_done = None
    for chunk in range(CHUNKS):
        a_out = list(pack(chunk, top, a_experts, a_rows))
        b_out = list(pack(chunk, top, b_experts, b_rows))
        a_experts, b_experts, a_out, b_out = lax.optimization_barrier(
            (a_experts, b_experts, a_out, b_out)
        )
        if chunk:
            b_out[2], a_done[0] = lax.optimization_barrier((b_out[2], a_done[0]))
        a_in = [a_out[0]] + [shift(a_out[k], "x", k) for k in range(1, SIDE)]
        b_in = [b_out[0]] + [shift(b_out[k], "z", k) for k in range(1, SIDE)]
        a_done, b_done = expert(w_gate, w_up, w_down, a_in, b_in)
        a_done = list(a_done)
        a_back.append([a_done[0]] + [shift(a_done[k], "x", -k) for k in range(1, SIDE)])
        b_back.append([b_done[0]] + [shift(b_done[k], "z", -k) for k in range(1, SIDE)])

    a_sums = sum_rows(top, a_experts, a_rows, sum(a_back, []))
    b_sums = sum_rows(top, b_experts, b_rows, sum(b_back, []))
    a_home = [a_sums[0]] + [shift(a_sums[k], "z", -k) for k in range(1, SIDE)]
    b_home = [b_sums[0]] + [shift(b_sums[k], "x", -k) for k in range(1, SIDE)]
    mixed = [sum(part.astype(jnp.float32) for part in home) for home in (a_home, b_home)]
    return jnp.concatenate(mixed, axis=1).astype(jnp.bfloat16)


def solution(mesh):
    dp = mesh.devices.shape[0]
    grid = Mesh(mesh.devices.reshape(dp, SIDE, SIDE), ("dp", "z", "x"))
    rows, experts = ("dp", "z", "x"), ("z", "x")
    in_specs = (
        P(rows, None),
        P(rows, None),
        P(rows, None),
        P(experts, None, None),
        P(experts, None, None),
        P(experts, None, None),
    )
    return jax.shard_map(
        local, mesh=grid, in_specs=in_specs, out_specs=P(rows, None), check_vma=False
    )
```

```python
import functools

import jax
import jax.numpy as jnp
from jax import lax
from jax.experimental import pallas as pl
from jax.experimental.pallas import tpu as pltpu
from jax.sharding import Mesh, PartitionSpec as P

SIDE = 4
CAP = 64
CHUNKS = 2
ROWS = CAP // CHUNKS
TILE = 128
PACK_TILE = 1024
FF_TILE = 256
D_TILE = 1024
SUM_TILE = 512
VMEM = 36 * 1024 * 1024


def shift(block, axis, step):
    return lax.ppermute(block, axis, [(i, (i + step) % SIDE) for i in range(SIDE)])


def both_ways(a_blocks, b_blocks, a_axis, b_axis, sign):
    a_moved, b_moved = list(a_blocks), list(b_blocks)
    for k in (1, 3, 2):
        a_moved[k] = shift(a_blocks[k], a_axis, sign * k)
        b_moved[k] = shift(b_blocks[k], b_axis, sign * k)
    return a_moved, b_moved


def prepare_kernel(token_ref, id_ref, gate_ref, a_ref, b_ref):
    tokens, depth = token_ref.shape
    half = depth // 2
    top = id_ref.shape[0]
    given = jnp.concatenate([id_ref[...].astype(jnp.float32), gate_ref[...]], axis=0).T
    lane = lax.broadcasted_iota(jnp.int32, (tokens, TILE), 1)
    number = lane.astype(jnp.float32)
    row = lax.broadcasted_iota(jnp.int32, (tokens, tokens), 0)
    column = lax.broadcasted_iota(jnp.int32, (tokens, tokens), 1)
    ids = [given[:, k : k + 1] for k in range(top)]
    named = jnp.zeros((tokens, TILE), jnp.float32)
    for k in range(top):
        named = jnp.where(ids[k] == number, 1.0, named)
    before = jnp.where(column < row, 1.0, 0.0).astype(jnp.bfloat16)
    rank = jnp.dot(before, named.astype(jnp.bfloat16), preferred_element_type=jnp.float32)
    facts = jnp.zeros((tokens, TILE), jnp.float32)
    for k in range(top):
        place = jnp.sum(jnp.where(ids[k] == number, rank, 0.0), axis=1, keepdims=True)
        facts = jnp.where(lane == k, ids[k], facts)
        facts = jnp.where(lane == top + k, place, facts)
        rest = given[:, top + k : top + k + 1]
        for part in range(2, 5):
            term = rest.astype(jnp.bfloat16).astype(jnp.float32)
            facts = jnp.where(lane == part * top + k, term, facts)
            rest = rest - term
    facts = facts.astype(jnp.bfloat16)
    a_ref[:, :half] = token_ref[:, :half]
    b_ref[:, :half] = token_ref[:, half:]
    a_ref[:, half:] = facts
    b_ref[:, half:] = facts


def prepare(tokens, expert_ids, gate_values):
    rows, depth = tokens.shape
    out = jax.ShapeDtypeStruct((rows, depth // 2 + TILE), jnp.bfloat16)
    return pl.pallas_call(
        prepare_kernel,
        out_shape=[out, out],
        compiler_params=pltpu.CompilerParams(vmem_limit_bytes=VMEM),
        cost_estimate=pl.CostEstimate(
            flops=2 * rows * rows * TILE, bytes_accessed=4 * rows * depth, transcendentals=0
        ),
    )(tokens, expert_ids.T, gate_values.T)


def codes(facts, top):
    facts = facts.astype(jnp.float32)
    return [facts[:, k : k + 1] * CAP + facts[:, top + k : top + k + 1] for k in range(top)]


def targets(places_ref, first, chunks, tokens):
    count = len(chunks) * SIDE * ROWS
    lane = lax.broadcasted_iota(jnp.int32, (tokens, count), 1)
    code = jnp.zeros((tokens, count), jnp.int32)
    for n, chunk in enumerate(chunks):
        for dest in range(SIDE):
            low = (n * SIDE + dest) * ROWS
            value = places_ref[first + dest] * CAP + chunk * ROWS + lane - low
            code = jnp.where((lane >= low) & (lane < low + ROWS), value, code)
    return code.astype(jnp.float32)


def pack_kernel(chunk, top, places_ref, *refs):
    sources, facts = refs[:SIDE], refs[SIDE : 2 * SIDE]
    outs, pick_ref = refs[2 * SIDE : -1], refs[-1]
    tokens = sources[0].shape[0]

    @pl.when(pl.program_id(0) == 0)
    def _():
        target = targets(places_ref, 0, (chunk,), tokens)
        for source in range(SIDE):
            pick = jnp.zeros(target.shape, jnp.float32)
            for code in codes(facts[source][...], top):
                pick = jnp.where(code == target, 1.0, pick)
            pick_ref[source] = pick.T.astype(jnp.bfloat16)

    for source in range(SIDE):
        rows = jnp.dot(
            pick_ref[source], sources[source][...], preferred_element_type=jnp.float32
        ).astype(jnp.bfloat16)
        for dest in range(SIDE):
            outs[dest][source] = rows[dest * ROWS : (dest + 1) * ROWS]


def wide_specs(tokens, tile):
    return [
        pl.BlockSpec((tokens, tile), lambda i, places, k=k: (places[SIDE + k], i))
        for k in range(SIDE)
    ]


def fact_specs(tokens, last):
    return [
        pl.BlockSpec((tokens, TILE), lambda i, places, k=k: (places[SIDE + k], last))
        for k in range(SIDE)
    ]


def pack(chunk, top, places, blocks):
    width = blocks[0].shape[1] - TILE
    tokens = blocks[-1].shape[0]
    if len(blocks) == 1:
        blocks, tokens = list(blocks) * SIDE, tokens // SIDE
    tile = min(PACK_TILE, width)
    out = jax.ShapeDtypeStruct((SIDE, ROWS, width), jnp.bfloat16)
    return pl.pallas_call(
        functools.partial(pack_kernel, chunk, top),
        grid_spec=pltpu.PrefetchScalarGridSpec(
            num_scalar_prefetch=1,
            grid=(width // tile,),
            in_specs=wide_specs(tokens, tile) + fact_specs(tokens, width // TILE),
            out_specs=[pl.BlockSpec((SIDE, ROWS, tile), lambda i, places: (0, 0, i))] * SIDE,
            scratch_shapes=[pltpu.VMEM((SIDE, SIDE * ROWS, tokens), jnp.bfloat16)],
        ),
        out_shape=[out] * SIDE,
        compiler_params=pltpu.CompilerParams(vmem_limit_bytes=VMEM),
        cost_estimate=pl.CostEstimate(
            flops=2 * SIDE * SIDE * ROWS * tokens * width,
            bytes_accessed=2 * SIDE * width * (tokens + SIDE * ROWS),
            transcendentals=0,
        ),
    )(places, *blocks, *blocks)


def expert_kernel(n_ff, n_half, wg_ref, wu_ref, wd_ref, *refs):
    a_in, b_in = refs[:SIDE], refs[SIDE : 2 * SIDE]
    a_out, b_out = refs[2 * SIDE : 3 * SIDE], refs[3 * SIDE : 4 * SIDE]
    x_ref, hidden_ref, sems = refs[4 * SIDE :]
    step = pl.program_id(0)
    half = x_ref.shape[-1] // 2
    count = SIDE * SIDE * ROWS

    @pl.when(step == 0)
    def _():
        copies = []
        for k in range(SIDE):
            copies.append(
                pltpu.make_async_copy(a_in[k], x_ref.at[:, k, :, :half], sems.at[k])
            )
            copies.append(
                pltpu.make_async_copy(b_in[k], x_ref.at[k, :, :, half:], sems.at[SIDE + k])
            )
        for copy in copies:
            copy.start()
        for copy in copies:
            copy.wait()

    for f in range(n_ff):

        @pl.when(step == f)
        def _(f=f):
            x = x_ref[...].reshape(count, 2 * half)
            gate = jnp.dot(x, wg_ref[...], preferred_element_type=jnp.float32)
            up = jnp.dot(x, wu_ref[...], preferred_element_type=jnp.float32)
            tile = gate.shape[1]
            hidden = gate / (1.0 + jnp.exp(-gate)) * up
            hidden_ref[:, f * tile : (f + 1) * tile] = hidden.astype(jnp.bfloat16)

    def down():
        out = jnp.dot(hidden_ref[...], wd_ref[...], preferred_element_type=jnp.float32)
        return out.astype(jnp.bfloat16).reshape(SIDE, SIDE, ROWS, out.shape[1])

    @pl.when((step >= n_ff) & (step < n_ff + n_half))
    def _():
        out = down()
        for k in range(SIDE):
            a_out[k][...] = out[:, k]

    @pl.when(step >= n_ff + n_half)
    def _():
        out = down()
        for k in range(SIDE):
            b_out[k][...] = out[k]


def expert(w_gate, w_up, w_down, a_in, b_in):
    half = a_in[0].shape[-1]
    depth, ff = w_gate.shape
    count = SIDE * SIDE * ROWS
    n_ff = ff // FF_TILE
    d_tile = min(D_TILE, half)
    n_half = half // d_tile
    ff_spec = pl.BlockSpec((depth, FF_TILE), lambda i: (0, jnp.minimum(i, n_ff - 1)))
    wd_spec = pl.BlockSpec((ff, d_tile), lambda i: (0, jnp.maximum(i - n_ff, 0)))
    a_spec = pl.BlockSpec(
        (SIDE, ROWS, d_tile), lambda i: (0, 0, jnp.clip(i - n_ff, 0, n_half - 1))
    )
    b_spec = pl.BlockSpec(
        (SIDE, ROWS, d_tile), lambda i: (0, 0, jnp.clip(i - n_ff - n_half, 0, n_half - 1))
    )
    out = jax.ShapeDtypeStruct((SIDE, ROWS, half), jnp.bfloat16)
    done = pl.pallas_call(
        functools.partial(expert_kernel, n_ff, n_half),
        grid=(n_ff + 2 * n_half,),
        in_specs=[ff_spec, ff_spec, wd_spec]
        + [pl.BlockSpec(memory_space=pl.ANY)] * (2 * SIDE),
        out_specs=[a_spec] * SIDE + [b_spec] * SIDE,
        out_shape=[out] * (2 * SIDE),
        scratch_shapes=[
            pltpu.VMEM((SIDE, SIDE, ROWS, depth), jnp.bfloat16),
            pltpu.VMEM((count, ff), jnp.bfloat16),
            pltpu.SemaphoreType.DMA((2 * SIDE,)),
        ],
        compiler_params=pltpu.CompilerParams(vmem_limit_bytes=VMEM),
        cost_estimate=pl.CostEstimate(
            flops=6 * count * depth * ff,
            bytes_accessed=6 * depth * ff + 4 * count * depth,
            transcendentals=count * ff,
        ),
    )(w_gate, w_up, w_down, *a_in, *b_in)
    return done[:SIDE], done[SIDE:]


def weigh(places_ref, first, top, facts, high_ref, low_ref):
    tokens = high_ref.shape[1]
    target = targets(places_ref, first, tuple(range(CHUNKS)), tokens)
    for source in range(SIDE):
        about = facts[source][...]
        wide = about.astype(jnp.float32)
        weight = jnp.zeros(target.shape, jnp.float32)
        for k, code in enumerate(codes(about, top)):
            one, two, three = (
                wide[:, part * top + k : part * top + k + 1] for part in range(2, 5)
            )
            weight = jnp.where(code == target, one + two + three, weight)
        high = weight.astype(jnp.bfloat16)
        high_ref[source] = high
        low_ref[source] = (weight - high.astype(jnp.float32)).astype(jnp.bfloat16)


def sum_kernel(top, places_ref, *refs):
    count = CHUNKS * SIDE
    a_in, b_in, refs = refs[:count], refs[count : 2 * count], refs[2 * count :]
    a_facts, b_facts, refs = refs[:SIDE], refs[SIDE : 2 * SIDE], refs[2 * SIDE :]
    a_out, b_out, (high_ref, low_ref) = refs[0], refs[1 : 1 + SIDE], refs[1 + SIDE :]

    @pl.when(pl.program_id(0) == 0)
    def _():
        weigh(places_ref, 0, top, a_facts, high_ref.at[0], low_ref.at[0])
        weigh(places_ref, 2 * SIDE, top, b_facts, high_ref.at[1], low_ref.at[1])

    def total(half, source, ins):
        rows = jnp.concatenate([ref[source] for ref in ins], axis=0)
        out = jnp.dot(high_ref[half, source], rows, preferred_element_type=jnp.float32)
        low = jnp.dot(low_ref[half, source], rows, preferred_element_type=jnp.float32)
        return (out + low).astype(jnp.bfloat16)

    for source in range(SIDE):
        a_out[places_ref[SIDE + source]] = total(0, source, a_in)
        b_out[source][...] = total(1, source, b_in)


def sum_rows(top, places, a_facts, b_facts, a_blocks, b_blocks):
    width = a_blocks[0].shape[-1]
    tokens = b_facts[0].shape[0]
    tile = min(SUM_TILE, width)
    last = width // TILE
    block = pl.BlockSpec((SIDE, ROWS, tile), lambda i, places: (0, 0, i))
    weights = pltpu.VMEM((2, SIDE, tokens, SIDE * CAP), jnp.bfloat16)
    done = pl.pallas_call(
        functools.partial(sum_kernel, top),
        grid_spec=pltpu.PrefetchScalarGridSpec(
            num_scalar_prefetch=1,
            grid=(width // tile,),
            in_specs=[block] * (len(a_blocks) + len(b_blocks))
            + fact_specs(tokens, last)
            + [pl.BlockSpec((tokens, TILE), lambda i, places: (0, last))] * SIDE,
            out_specs=[pl.BlockSpec((SIDE, tokens, tile), lambda i, places: (0, 0, i))]
            + [pl.BlockSpec((tokens, tile), lambda i, places: (0, i))] * SIDE,
            scratch_shapes=[weights, weights],
        ),
        out_shape=[pltpu.HBM((SIDE, tokens, width), jnp.bfloat16)]
        + [jax.ShapeDtypeStruct((tokens, width), jnp.bfloat16)] * SIDE,
        compiler_params=pltpu.CompilerParams(vmem_limit_bytes=VMEM),
        cost_estimate=pl.CostEstimate(
            flops=8 * SIDE * SIDE * CAP * tokens * width,
            bytes_accessed=4 * SIDE * width * (tokens + SIDE * CAP),
            transcendentals=0,
        ),
    )(places, *a_blocks, *b_blocks, *[a_facts] * SIDE, *b_facts)
    return done[0], done[1:]


def local(tokens, expert_ids, gate_values, gate_weight, up_weight, down_weight):
    count, top = expert_ids.shape
    z, x = lax.axis_index("z"), lax.axis_index("x")
    steps = jnp.arange(SIDE, dtype=jnp.int32)
    a_places = jnp.concatenate([z * SIDE + (x + steps) % SIDE, (z - steps) % SIDE])
    b_places = jnp.concatenate([(z + steps) % SIDE * SIDE + x, steps * 0])

    a_half, b_half = prepare(tokens, expert_ids, gate_values)
    a_rows = lax.all_gather(a_half, "z", axis=0, tiled=True)
    a_rows = pltpu.with_memory_space_constraint(a_rows, pltpu.HBM)
    b_rows = [b_half] + [shift(b_half, "x", k) for k in range(1, SIDE)]

    weights = gate_weight[0], up_weight[0], down_weight[0]
    weights = [pltpu.with_memory_space_constraint(w, pltpu.HBM) for w in weights]
    a_back, b_back = [], []
    a_done = None
    for chunk in range(CHUNKS):
        a_out = list(pack(chunk, top, a_places, [a_rows]))
        b_out = list(pack(chunk, top, b_places, b_rows))
        a_places, b_places, a_out, b_out = lax.optimization_barrier(
            (a_places, b_places, a_out, b_out)
        )
        if chunk:
            b_out[2], a_done[0] = lax.optimization_barrier((b_out[2], a_done[0]))
        a_in, b_in = both_ways(a_out, b_out, "x", "z", 1)
        a_done, b_done = expert(*weights, a_in, b_in)
        a_done = list(a_done)
        a_home, b_home = both_ways(a_done, b_done, "x", "z", -1)
        a_back += a_home
        b_back += b_home

    places = jnp.concatenate([a_places, b_places])
    a_sums, b_sums = sum_rows(top, places, a_rows, b_rows, a_back, b_back)
    a_mixed = lax.psum_scatter(
        a_sums.reshape(SIDE * count, -1), "z", scatter_dimension=0, tiled=True
    )
    b_home = [b_sums[0]] + [shift(b_sums[k], "x", -k) for k in range(1, SIDE)]
    b_mixed = sum(part.astype(jnp.float32) for part in b_home).astype(jnp.bfloat16)
    return jnp.concatenate([a_mixed, b_mixed], axis=1)


def solution(mesh):
    dp = mesh.devices.shape[0]
    grid = Mesh(mesh.devices.reshape(dp, SIDE, SIDE), ("dp", "z", "x"))
    rows, experts = ("dp", "z", "x"), ("z", "x")
    in_specs = (
        P(rows, None),
        P(rows, None),
        P(rows, None),
        P(experts, None, None),
        P(experts, None, None),
        P(experts, None, None),
    )
    return jax.shard_map(
        local, mesh=grid, in_specs=in_specs, out_specs=P(rows, None), check_vma=False
    )
```

```python
import functools

import jax
import jax.numpy as jnp
from jax import lax
from jax.experimental import pallas as pl
from jax.experimental.pallas import tpu as pltpu
from jax.sharding import Mesh, PartitionSpec as P

SIDE = 4
CAP = 64
CHUNKS = 2
ROWS = CAP // CHUNKS
TILE = 128
FF_TILE = 256
D_TILE = 1024
VMEM = 36 * 1024 * 1024


def shift(block, axis, step):
    return lax.ppermute(block, axis, [(i, (i + step) % SIDE) for i in range(SIDE)])


def gather_line(half, axis):
    rows = half.shape[0] // 2
    if axis == "z":
        ahead, behind = shift(half, axis, 1), shift(half, axis, 3)
        return [half, ahead, shift(half, axis, 2), behind]
    ahead, behind = shift(half, axis, 1), shift(half, axis, -1)
    low = shift(ahead[:rows], axis, 1)
    high = shift(behind[rows:], axis, -1)
    return [half, ahead, low, high, behind]


def line_rows(refs, column=slice(None)):
    if len(refs) == SIDE:
        return [ref[:, column] for ref in refs]
    own, ahead, low, high, behind = [ref[:, column] for ref in refs]
    return [own, ahead, jnp.concatenate([low, high], axis=0), behind]


def both_ways(a_blocks, b_blocks, a_axis, b_axis, sign):
    a_moved, b_moved = list(a_blocks), list(b_blocks)
    for k in (1, 3, 2):
        a_moved[k] = shift(a_blocks[k], a_axis, sign * k)
        b_moved[k] = shift(b_blocks[k], b_axis, sign * k)
    return a_moved, b_moved


def prepare_kernel(token_ref, id_ref, gate_ref, a_ref, b_ref):
    tokens, depth = token_ref.shape
    half = depth // 2
    top = id_ref.shape[0]
    given = jnp.concatenate([id_ref[...].astype(jnp.float32), gate_ref[...]], axis=0).T
    lane = lax.broadcasted_iota(jnp.int32, (tokens, TILE), 1)
    number = lane.astype(jnp.float32)
    row = lax.broadcasted_iota(jnp.int32, (tokens, tokens), 0)
    column = lax.broadcasted_iota(jnp.int32, (tokens, tokens), 1)
    ids = [given[:, k : k + 1] for k in range(top)]
    named = jnp.zeros((tokens, TILE), jnp.float32)
    for k in range(top):
        named = jnp.where(ids[k] == number, 1.0, named)
    before = jnp.where(column < row, 1.0, 0.0).astype(jnp.bfloat16)
    rank = jnp.dot(before, named.astype(jnp.bfloat16), preferred_element_type=jnp.float32)
    facts = jnp.zeros((tokens, TILE), jnp.float32)
    for k in range(top):
        place = jnp.sum(jnp.where(ids[k] == number, rank, 0.0), axis=1, keepdims=True)
        facts = jnp.where(lane == k, ids[k], facts)
        facts = jnp.where(lane == top + k, place, facts)
        facts = jnp.where(lane == 2 * top + k, given[:, top + k : top + k + 1], facts)
    facts = facts.astype(jnp.bfloat16)
    a_ref[:, :half] = token_ref[:, :half]
    b_ref[:, :half] = token_ref[:, half:]
    a_ref[:, half:] = facts
    b_ref[:, half:] = facts


def prepare(tokens, expert_ids, gate_values):
    rows, depth = tokens.shape
    out = jax.ShapeDtypeStruct((rows, depth // 2 + TILE), jnp.bfloat16)
    return pl.pallas_call(
        prepare_kernel,
        out_shape=[out, out],
        compiler_params=pltpu.CompilerParams(vmem_limit_bytes=VMEM),
        cost_estimate=pl.CostEstimate(
            flops=2 * rows * rows * TILE, bytes_accessed=4 * rows * depth, transcendentals=0
        ),
    )(tokens, expert_ids.T, gate_values.T)


def codes(facts, top):
    facts = facts.astype(jnp.float32)
    return [facts[:, k : k + 1] * CAP + facts[:, top + k : top + k + 1] for k in range(top)]


def targets(experts_ref, first, chunks, tokens):
    count = len(chunks) * SIDE * ROWS
    lane = lax.broadcasted_iota(jnp.int32, (tokens, count), 1)
    code = jnp.zeros((tokens, count), jnp.int32)
    for n, chunk in enumerate(chunks):
        for dest in range(SIDE):
            low = (n * SIDE + dest) * ROWS
            value = experts_ref[first + dest] * CAP + chunk * ROWS + lane - low
            code = jnp.where((lane >= low) & (lane < low + ROWS), value, code)
    return code.astype(jnp.float32)


def pack_kernel(chunk, top, experts_ref, *refs):
    blocks, outs = refs[:-SIDE], refs[-SIDE:]
    tokens = blocks[0].shape[0]
    width = outs[0].shape[-1]
    target = targets(experts_ref, 0, (chunk,), tokens)
    facts = line_rows(blocks, slice(width, width + TILE))
    rows_in = line_rows(blocks, slice(0, width))
    for source in range(SIDE):
        pick = jnp.zeros(target.shape, jnp.float32)
        for code in codes(facts[source], top):
            pick = jnp.where(code == target, 1.0, pick)
        rows = jnp.dot(
            pick.T.astype(jnp.bfloat16), rows_in[source], preferred_element_type=jnp.float32
        ).astype(jnp.bfloat16)
        for dest in range(SIDE):
            outs[dest][source] = rows[dest * ROWS : (dest + 1) * ROWS]


def pack(chunk, top, experts, blocks):
    tokens, width = blocks[0].shape
    width -= TILE
    out = jax.ShapeDtypeStruct((SIDE, ROWS, width), jnp.bfloat16)
    return pl.pallas_call(
        functools.partial(pack_kernel, chunk, top),
        in_specs=[pl.BlockSpec(memory_space=pltpu.SMEM)]
        + [pl.BlockSpec(memory_space=pltpu.VMEM)] * len(blocks),
        out_specs=[pl.BlockSpec(memory_space=pltpu.VMEM)] * SIDE,
        out_shape=[out] * SIDE,
        compiler_params=pltpu.CompilerParams(vmem_limit_bytes=VMEM),
        cost_estimate=pl.CostEstimate(
            flops=2 * SIDE * SIDE * ROWS * tokens * width,
            bytes_accessed=2 * SIDE * width * (tokens + SIDE * ROWS),
            transcendentals=0,
        ),
    )(experts, *blocks)


def expert_kernel(n_ff, n_half, wg_ref, wu_ref, wd_ref, *refs):
    a_in, b_in = refs[:SIDE], refs[SIDE : 2 * SIDE]
    a_out, b_out = refs[2 * SIDE : 3 * SIDE], refs[3 * SIDE : 4 * SIDE]
    x_ref, hidden_ref, sems = refs[4 * SIDE :]
    step = pl.program_id(0)
    half = x_ref.shape[-1] // 2
    count = SIDE * SIDE * ROWS

    @pl.when(step == 0)
    def _():
        copies = []
        for k in range(SIDE):
            copies.append(
                pltpu.make_async_copy(a_in[k], x_ref.at[:, k, :, :half], sems.at[k])
            )
            copies.append(
                pltpu.make_async_copy(b_in[k], x_ref.at[k, :, :, half:], sems.at[SIDE + k])
            )
        for copy in copies:
            copy.start()
        for copy in copies:
            copy.wait()

    for f in range(n_ff):

        @pl.when(step == f)
        def _(f=f):
            x = x_ref[...].reshape(count, 2 * half)
            gate = jnp.dot(x, wg_ref[...], preferred_element_type=jnp.float32)
            up = jnp.dot(x, wu_ref[...], preferred_element_type=jnp.float32)
            tile = gate.shape[1]
            hidden = gate / (1.0 + jnp.exp(-gate)) * up
            hidden_ref[:, f * tile : (f + 1) * tile] = hidden.astype(jnp.bfloat16)

    def down():
        out = jnp.dot(hidden_ref[...], wd_ref[...], preferred_element_type=jnp.float32)
        return out.astype(jnp.bfloat16).reshape(SIDE, SIDE, ROWS, out.shape[1])

    @pl.when((step >= n_ff) & (step < n_ff + n_half))
    def _():
        out = down()
        for k in range(SIDE):
            a_out[k][...] = out[:, k]

    @pl.when(step >= n_ff + n_half)
    def _():
        out = down()
        for k in range(SIDE):
            b_out[k][...] = out[k]


def expert(w_gate, w_up, w_down, a_in, b_in):
    half = a_in[0].shape[-1]
    depth, ff = w_gate.shape
    count = SIDE * SIDE * ROWS
    n_ff = ff // FF_TILE
    d_tile = min(D_TILE, half)
    n_half = half // d_tile
    ff_spec = pl.BlockSpec((depth, FF_TILE), lambda i: (0, jnp.minimum(i, n_ff - 1)))
    wd_spec = pl.BlockSpec((ff, d_tile), lambda i: (0, jnp.maximum(i - n_ff, 0)))
    a_spec = pl.BlockSpec(
        (SIDE, ROWS, d_tile), lambda i: (0, 0, jnp.clip(i - n_ff, 0, n_half - 1))
    )
    b_spec = pl.BlockSpec(
        (SIDE, ROWS, d_tile), lambda i: (0, 0, jnp.clip(i - n_ff - n_half, 0, n_half - 1))
    )
    out = jax.ShapeDtypeStruct((SIDE, ROWS, half), jnp.bfloat16)
    done = pl.pallas_call(
        functools.partial(expert_kernel, n_ff, n_half),
        grid=(n_ff + 2 * n_half,),
        in_specs=[ff_spec, ff_spec, wd_spec]
        + [pl.BlockSpec(memory_space=pl.ANY)] * (2 * SIDE),
        out_specs=[a_spec] * SIDE + [b_spec] * SIDE,
        out_shape=[out] * (2 * SIDE),
        scratch_shapes=[
            pltpu.VMEM((SIDE, SIDE, ROWS, depth), jnp.bfloat16),
            pltpu.VMEM((count, ff), jnp.bfloat16),
            pltpu.SemaphoreType.DMA((2 * SIDE,)),
        ],
        compiler_params=pltpu.CompilerParams(vmem_limit_bytes=VMEM),
        cost_estimate=pl.CostEstimate(
            flops=6 * count * depth * ff,
            bytes_accessed=6 * depth * ff + 4 * count * depth,
            transcendentals=count * ff,
        ),
    )(w_gate, w_up, w_down, *a_in, *b_in)
    return done[:SIDE], done[SIDE:]


def sum_kernel(top, counts, experts_ref, *refs):
    groups = []
    for count in counts:
        groups.append(refs[:count])
        refs = refs[count:]
    a_in, b_in, a_facts, b_facts, a_out, b_out = groups
    tokens = a_out[0].shape[0]
    for first, ins, blocks, outs in ((0, a_in, a_facts, a_out), (SIDE, b_in, b_facts, b_out)):
        target = targets(experts_ref, first, tuple(range(CHUNKS)), tokens)
        facts = line_rows(blocks)
        for source in range(SIDE):
            wide = facts[source].astype(jnp.float32)
            weight = jnp.zeros(target.shape, jnp.float32)
            for k, code in enumerate(codes(wide, top)):
                gate = wide[:, 2 * top + k : 2 * top + k + 1]
                weight = jnp.where(code == target, gate, weight)
            rows = jnp.concatenate([ref[source] for ref in ins], axis=0)
            total = jnp.dot(
                weight.astype(jnp.bfloat16), rows, preferred_element_type=jnp.float32
            )
            outs[source][...] = total.astype(jnp.bfloat16)


def sum_rows(top, experts, a_facts, b_facts, a_blocks, b_blocks):
    width = a_blocks[0].shape[-1]
    tokens = a_facts[0].shape[0]
    facts = [*a_facts, *b_facts]
    last = width // TILE
    whole = pl.BlockSpec(memory_space=pltpu.VMEM)
    out = jax.ShapeDtypeStruct((tokens, width), jnp.bfloat16)
    counts = (len(a_blocks), len(b_blocks), len(a_facts), len(b_facts), SIDE, SIDE)
    done = pl.pallas_call(
        functools.partial(sum_kernel, top, counts),
        grid=(1,),
        in_specs=[pl.BlockSpec(memory_space=pltpu.SMEM)]
        + [whole] * (len(a_blocks) + len(b_blocks))
        + [pl.BlockSpec((f.shape[0], TILE), lambda i: (0, last)) for f in facts],
        out_specs=[whole] * (2 * SIDE),
        out_shape=[out] * (2 * SIDE),
        compiler_params=pltpu.CompilerParams(vmem_limit_bytes=VMEM),
        cost_estimate=pl.CostEstimate(
            flops=4 * SIDE * SIDE * CAP * tokens * width,
            bytes_accessed=4 * SIDE * width * (tokens + SIDE * CAP),
            transcendentals=0,
        ),
    )(experts, *a_blocks, *b_blocks, *facts)
    return done[:SIDE], done[SIDE:]


def local(tokens, expert_ids, gate_values, gate_weight, up_weight, down_weight):
    top = expert_ids.shape[1]
    z, x = lax.axis_index("z"), lax.axis_index("x")
    steps = jnp.arange(SIDE, dtype=jnp.int32)
    a_experts = z * SIDE + (x + steps) % SIDE
    b_experts = (z + steps) % SIDE * SIDE + x

    a_half, b_half = prepare(tokens, expert_ids, gate_values)
    b_rows = gather_line(b_half, "x")
    a_rows = gather_line(a_half, "z")

    weights = gate_weight[0], up_weight[0], down_weight[0]
    weights = [pltpu.with_memory_space_constraint(w, pltpu.HBM) for w in weights]
    a_back, b_back = [], []
    a_done = None
    for chunk in range(CHUNKS):
        a_out = list(pack(chunk, top, a_experts, a_rows))
        b_out = list(pack(chunk, top, b_experts, b_rows))
        a_experts, b_experts, a_out, b_out = lax.optimization_barrier(
            (a_experts, b_experts, a_out, b_out)
        )
        if chunk:
            b_out[2], a_done[0] = lax.optimization_barrier((b_out[2], a_done[0]))
        a_in, b_in = both_ways(a_out, b_out, "x", "z", 1)
        a_done, b_done = expert(*weights, a_in, b_in)
        a_done = list(a_done)
        a_home, b_home = both_ways(a_done, b_done, "x", "z", -1)
        a_back += a_home
        b_back += b_home

    experts = jnp.concatenate([a_experts, b_experts])
    a_sums, b_sums = sum_rows(top, experts, a_rows, b_rows, a_back, b_back)
    a_home, b_home = both_ways(a_sums, b_sums, "z", "x", -1)
    mixed = [sum(part.astype(jnp.float32) for part in home) for home in (a_home, b_home)]
    return jnp.concatenate(mixed, axis=1).astype(jnp.bfloat16)


def solution(mesh):
    dp = mesh.devices.shape[0]
    grid = Mesh(mesh.devices.reshape(dp, SIDE, SIDE), ("dp", "z", "x"))
    rows, experts = ("dp", "z", "x"), ("z", "x")
    in_specs = (
        P(rows, None),
        P(rows, None),
        P(rows, None),
        P(experts, None, None),
        P(experts, None, None),
        P(experts, None, None),
    )
    return jax.shard_map(
        local, mesh=grid, in_specs=in_specs, out_specs=P(rows, None), check_vma=False
    )
```

```python
import functools

import jax
import jax.numpy as jnp
from jax import lax
from jax.experimental import pallas as pl
from jax.experimental.pallas import tpu as pltpu
from jax.sharding import Mesh, PartitionSpec as P

SIDE = 4
CAP = 64
CHUNKS = 2
ROWS = CAP // CHUNKS
TILE = 128
FF_TILE = 256
D_TILE = 1024
VMEM = 36 * 1024 * 1024


def shift(block, axis, step):
    return lax.ppermute(block, axis, [(i, (i + step) % SIDE) for i in range(SIDE)])


def gather_line(half, axis):
    rows = half.shape[0] // 2
    ahead, behind = shift(half, axis, 1), shift(half, axis, -1)
    low = shift(ahead[:rows], axis, 1)
    high = shift(behind[rows:], axis, -1)
    return [half, ahead, low, high, behind]


def line_rows(refs, column=slice(None)):
    own, ahead, low, high, behind = [ref[:, column] for ref in refs]
    return [own, ahead, jnp.concatenate([low, high], axis=0), behind]


def both_ways(a_blocks, b_blocks, a_axis, b_axis, sign):
    a_moved, b_moved = list(a_blocks), list(b_blocks)
    for k in (1, 3, 2):
        a_moved[k] = shift(a_blocks[k], a_axis, sign * k)
        b_moved[k] = shift(b_blocks[k], b_axis, sign * k)
    return a_moved, b_moved


def in_hbm(*arrays):
    return [pltpu.with_memory_space_constraint(array, pltpu.HBM) for array in arrays]


def prepare_kernel(token_ref, id_ref, gate_ref, a_ref, b_ref):
    tokens, depth = token_ref.shape
    half = depth // 2
    top = id_ref.shape[0]
    given = jnp.concatenate([id_ref[...].astype(jnp.float32), gate_ref[...]], axis=0).T
    lane = lax.broadcasted_iota(jnp.int32, (tokens, TILE), 1)
    number = lane.astype(jnp.float32)
    row = lax.broadcasted_iota(jnp.int32, (tokens, tokens), 0)
    column = lax.broadcasted_iota(jnp.int32, (tokens, tokens), 1)
    ids = [given[:, k : k + 1] for k in range(top)]
    named = jnp.zeros((tokens, TILE), jnp.float32)
    for k in range(top):
        named = jnp.where(ids[k] == number, 1.0, named)
    before = jnp.where(column < row, 1.0, 0.0).astype(jnp.bfloat16)
    rank = jnp.dot(before, named.astype(jnp.bfloat16), preferred_element_type=jnp.float32)
    facts = jnp.zeros((tokens, TILE), jnp.float32)
    for k in range(top):
        place = jnp.sum(jnp.where(ids[k] == number, rank, 0.0), axis=1, keepdims=True)
        facts = jnp.where(lane == k, ids[k], facts)
        facts = jnp.where(lane == top + k, place, facts)
        facts = jnp.where(lane == 2 * top + k, given[:, top + k : top + k + 1], facts)
    facts = facts.astype(jnp.bfloat16)
    a_ref[:, :half] = token_ref[:, :half]
    b_ref[:, :half] = token_ref[:, half:]
    a_ref[:, half:] = facts
    b_ref[:, half:] = facts


def prepare(tokens, expert_ids, gate_values):
    rows, depth = tokens.shape
    out = jax.ShapeDtypeStruct((rows, depth // 2 + TILE), jnp.bfloat16)
    top = expert_ids.shape[1]
    return pl.pallas_call(
        prepare_kernel,
        grid=(1,),
        in_specs=[
            pl.BlockSpec((rows, depth), lambda i: (0, 0)),
            pl.BlockSpec((top, rows), lambda i: (0, 0)),
            pl.BlockSpec((top, rows), lambda i: (0, 0)),
        ],
        out_specs=[pl.BlockSpec(out.shape, lambda i: (0, 0))] * 2,
        out_shape=[out, out],
        compiler_params=pltpu.CompilerParams(vmem_limit_bytes=VMEM),
        cost_estimate=pl.CostEstimate(
            flops=2 * rows * rows * TILE, bytes_accessed=4 * rows * depth, transcendentals=0
        ),
    )(*in_hbm(tokens, expert_ids.T, gate_values.T))


def codes(facts, top):
    facts = facts.astype(jnp.float32)
    return [facts[:, k : k + 1] * CAP + facts[:, top + k : top + k + 1] for k in range(top)]


def targets(experts_ref, first, chunks, tokens):
    count = len(chunks) * SIDE * ROWS
    lane = lax.broadcasted_iota(jnp.int32, (tokens, count), 1)
    code = jnp.zeros((tokens, count), jnp.int32)
    for n, chunk in enumerate(chunks):
        for dest in range(SIDE):
            low = (n * SIDE + dest) * ROWS
            value = experts_ref[first + dest] * CAP + chunk * ROWS + lane - low
            code = jnp.where((lane >= low) & (lane < low + ROWS), value, code)
    return code.astype(jnp.float32)


def pack_kernel(chunk, top, experts_ref, *refs):
    blocks, outs = refs[:-SIDE], refs[-SIDE:]
    tokens = blocks[0].shape[0]
    width = outs[0].shape[-1]
    target = targets(experts_ref, 0, (chunk,), tokens)
    facts = line_rows(blocks, slice(width, width + TILE))
    rows_in = line_rows(blocks, slice(0, width))
    for source in range(SIDE):
        pick = jnp.zeros(target.shape, jnp.float32)
        for code in codes(facts[source], top):
            pick = jnp.where(code == target, 1.0, pick)
        rows = jnp.dot(
            pick.T.astype(jnp.bfloat16), rows_in[source], preferred_element_type=jnp.float32
        ).astype(jnp.bfloat16)
        for dest in range(SIDE):
            outs[dest][source] = rows[dest * ROWS : (dest + 1) * ROWS]


def pack(chunk, top, experts, blocks):
    tokens, width = blocks[0].shape
    width -= TILE
    out = jax.ShapeDtypeStruct((SIDE, ROWS, width), jnp.bfloat16)
    return pl.pallas_call(
        functools.partial(pack_kernel, chunk, top),
        in_specs=[pl.BlockSpec(memory_space=pltpu.SMEM)]
        + [pl.BlockSpec(memory_space=pltpu.VMEM)] * len(blocks),
        out_specs=[pl.BlockSpec(memory_space=pltpu.VMEM)] * SIDE,
        out_shape=[out] * SIDE,
        compiler_params=pltpu.CompilerParams(vmem_limit_bytes=VMEM),
        cost_estimate=pl.CostEstimate(
            flops=2 * SIDE * SIDE * ROWS * tokens * width,
            bytes_accessed=2 * SIDE * width * (tokens + SIDE * ROWS),
            transcendentals=0,
        ),
    )(experts, *blocks)


def hidden_kernel(wg_ref, wu_ref, *refs):
    a_in, b_in = refs[:SIDE], refs[SIDE : 2 * SIDE]
    hidden_ref, x_ref, sems = refs[2 * SIDE :]
    half = x_ref.shape[-1] // 2
    count = SIDE * SIDE * ROWS

    @pl.when(pl.program_id(0) == 0)
    def _():
        copies = []
        for k in range(SIDE):
            copies.append(
                pltpu.make_async_copy(a_in[k], x_ref.at[:, k, :, :half], sems.at[k])
            )
            copies.append(
                pltpu.make_async_copy(b_in[k], x_ref.at[k, :, :, half:], sems.at[SIDE + k])
            )
        for copy in copies:
            copy.start()
        for copy in copies:
            copy.wait()

    x = x_ref[...].reshape(count, 2 * half)
    gate = jnp.dot(x, wg_ref[...], preferred_element_type=jnp.float32)
    up = jnp.dot(x, wu_ref[...], preferred_element_type=jnp.float32)
    hidden_ref[...] = (gate / (1.0 + jnp.exp(-gate)) * up).astype(jnp.bfloat16)


def hidden_rows(w_gate, w_up, a_in, b_in):
    depth, ff = w_gate.shape
    count = SIDE * SIDE * ROWS
    weight = pl.BlockSpec((depth, FF_TILE), lambda i: (0, i))
    return pl.pallas_call(
        hidden_kernel,
        grid=(ff // FF_TILE,),
        in_specs=[weight, weight] + [pl.BlockSpec(memory_space=pl.ANY)] * (2 * SIDE),
        out_specs=pl.BlockSpec((count, FF_TILE), lambda i: (0, i)),
        out_shape=jax.ShapeDtypeStruct((count, ff), jnp.bfloat16),
        scratch_shapes=[
            pltpu.VMEM((SIDE, SIDE, ROWS, depth), jnp.bfloat16),
            pltpu.SemaphoreType.DMA((2 * SIDE,)),
        ],
        compiler_params=pltpu.CompilerParams(vmem_limit_bytes=VMEM),
        cost_estimate=pl.CostEstimate(
            flops=4 * count * depth * ff,
            bytes_accessed=4 * depth * ff + 2 * count * depth,
            transcendentals=count * ff,
        ),
    )(w_gate, w_up, *a_in, *b_in)


def down_kernel(n_half, hidden_ref, wd_ref, *refs):
    a_out, b_out = refs[:SIDE], refs[SIDE:]
    out = jnp.dot(hidden_ref[...], wd_ref[...], preferred_element_type=jnp.float32)
    out = out.astype(jnp.bfloat16).reshape(SIDE, SIDE, ROWS, out.shape[1])

    @pl.when(pl.program_id(0) < n_half)
    def _():
        for k in range(SIDE):
            a_out[k][...] = out[:, k]

    @pl.when(pl.program_id(0) >= n_half)
    def _():
        for k in range(SIDE):
            b_out[k][...] = out[k]


def down_rows(hidden, w_down):
    count, ff = hidden.shape
    half = w_down.shape[1] // 2
    tile = min(D_TILE, half)
    n_half = half // tile
    a_spec = pl.BlockSpec((SIDE, ROWS, tile), lambda i: (0, 0, jnp.minimum(i, n_half - 1)))
    b_spec = pl.BlockSpec((SIDE, ROWS, tile), lambda i: (0, 0, jnp.maximum(i - n_half, 0)))
    out = jax.ShapeDtypeStruct((SIDE, ROWS, half), jnp.bfloat16)
    done = pl.pallas_call(
        functools.partial(down_kernel, n_half),
        grid=(2 * n_half,),
        in_specs=[
            pl.BlockSpec((count, ff), lambda i: (0, 0)),
            pl.BlockSpec((ff, tile), lambda i: (0, i)),
        ],
        out_specs=[a_spec] * SIDE + [b_spec] * SIDE,
        out_shape=[out] * (2 * SIDE),
        compiler_params=pltpu.CompilerParams(vmem_limit_bytes=VMEM),
        cost_estimate=pl.CostEstimate(
            flops=4 * count * half * ff,
            bytes_accessed=4 * half * ff + 4 * count * half,
            transcendentals=0,
        ),
    )(hidden, w_down)
    return done[:SIDE], done[SIDE:]


def sum_kernel(top, counts, experts_ref, *refs):
    groups = []
    for count in counts:
        groups.append(refs[:count])
        refs = refs[count:]
    a_in, b_in, a_facts, b_facts, a_out, b_out = groups
    tokens = a_out[0].shape[0]
    for first, ins, blocks, outs in ((0, a_in, a_facts, a_out), (SIDE, b_in, b_facts, b_out)):
        target = targets(experts_ref, first, tuple(range(CHUNKS)), tokens)
        facts = line_rows(blocks)
        for source in range(SIDE):
            wide = facts[source].astype(jnp.float32)
            weight = jnp.zeros(target.shape, jnp.float32)
            for k, code in enumerate(codes(wide, top)):
                gate = wide[:, 2 * top + k : 2 * top + k + 1]
                weight = jnp.where(code == target, gate, weight)
            rows = jnp.concatenate([ref[source] for ref in ins], axis=0)
            total = jnp.dot(
                weight.astype(jnp.bfloat16), rows, preferred_element_type=jnp.float32
            )
            outs[source][...] = total.astype(jnp.bfloat16)


def sum_rows(top, experts, a_facts, b_facts, a_blocks, b_blocks):
    width = a_blocks[0].shape[-1]
    tokens = a_facts[0].shape[0]
    facts = [*a_facts, *b_facts]
    last = width // TILE
    whole = pl.BlockSpec(memory_space=pltpu.VMEM)
    out = jax.ShapeDtypeStruct((tokens, width), jnp.bfloat16)
    counts = (len(a_blocks), len(b_blocks), len(a_facts), len(b_facts), SIDE, SIDE)
    done = pl.pallas_call(
        functools.partial(sum_kernel, top, counts),
        grid=(1,),
        in_specs=[pl.BlockSpec(memory_space=pltpu.SMEM)]
        + [whole] * (len(a_blocks) + len(b_blocks))
        + [pl.BlockSpec((f.shape[0], TILE), lambda i: (0, last)) for f in facts],
        out_specs=[whole] * (2 * SIDE),
        out_shape=[out] * (2 * SIDE),
        compiler_params=pltpu.CompilerParams(vmem_limit_bytes=VMEM),
        cost_estimate=pl.CostEstimate(
            flops=4 * SIDE * SIDE * CAP * tokens * width,
            bytes_accessed=4 * SIDE * width * (tokens + SIDE * CAP),
            transcendentals=0,
        ),
    )(experts, *a_blocks, *b_blocks, *facts)
    return done[:SIDE], done[SIDE:]


def local(tokens, expert_ids, gate_values, gate_weight, up_weight, down_weight):
    top = expert_ids.shape[1]
    z, x = lax.axis_index("z"), lax.axis_index("x")
    steps = jnp.arange(SIDE, dtype=jnp.int32)
    a_experts = z * SIDE + (x + steps) % SIDE
    b_experts = (z + steps) % SIDE * SIDE + x

    a_half, b_half = prepare(tokens, expert_ids, gate_values)
    b_rows = gather_line(b_half, "x")
    a_rows = gather_line(a_half, "z")

    w_gate, w_up, w_down = in_hbm(gate_weight[0], up_weight[0], down_weight[0])
    a_back, b_back = [], []
    for chunk in range(CHUNKS):
        a_out = list(pack(chunk, top, a_experts, a_rows))
        b_out = list(pack(chunk, top, b_experts, b_rows))
        a_experts, b_experts, a_out, b_out = lax.optimization_barrier(
            (a_experts, b_experts, a_out, b_out)
        )
        if chunk:
            b_out[2], hidden = lax.optimization_barrier((b_out[2], hidden))
            a_done, b_done = down_rows(hidden, w_down)
            a_home, b_home = both_ways(a_done, b_done, "x", "z", -1)
            a_back += a_home
            b_back += b_home
        a_in, b_in = both_ways(a_out, b_out, "x", "z", 1)
        hidden = hidden_rows(w_gate, w_up, a_in, b_in)
    hidden, a_back[1] = lax.optimization_barrier((hidden, a_back[1]))
    a_done, b_done = down_rows(hidden, w_down)
    a_home, b_home = both_ways(a_done, b_done, "x", "z", -1)
    a_back += a_home
    b_back += b_home

    experts = jnp.concatenate([a_experts, b_experts])
    a_sums, b_sums = sum_rows(top, experts, a_rows, b_rows, a_back, b_back)
    a_home, b_home = both_ways(a_sums, b_sums, "z", "x", -1)
    mixed = [sum(part.astype(jnp.float32) for part in home) for home in (a_home, b_home)]
    return jnp.concatenate(mixed, axis=1).astype(jnp.bfloat16)


def solution(mesh):
    dp = mesh.devices.shape[0]
    grid = Mesh(mesh.devices.reshape(dp, SIDE, SIDE), ("dp", "z", "x"))
    rows, experts = ("dp", "z", "x"), ("z", "x")
    in_specs = (
        P(rows, None),
        P(rows, None),
        P(rows, None),
        P(experts, None, None),
        P(experts, None, None),
        P(experts, None, None),
    )
    return jax.shard_map(
        local, mesh=grid, in_specs=in_specs, out_specs=P(rows, None), check_vma=False
    )
```

```python
import functools

import jax
import jax.numpy as jnp
from jax import lax
from jax.experimental import pallas as pl
from jax.experimental.pallas import tpu as pltpu
from jax.sharding import Mesh, PartitionSpec as P

SIDE = 4
CAP = 64
EARLY = 48
PLAN = (
    ((0, 0, EARLY), (1, 0, EARLY), (3, 0, EARLY)),
    ((0, EARLY, CAP - EARLY), (1, EARLY, CAP - EARLY), (3, EARLY, CAP - EARLY), (2, 0, CAP)),
)
TILE = 128
FF_TILE = 256
D_TILE = 1024
VMEM = 36 * 1024 * 1024


def shift(block, axis, step):
    return lax.ppermute(block, axis, [(i, (i + step) % SIDE) for i in range(SIDE)])


def gather_line(half, axis):
    rows = half.shape[0] // 2
    ahead, behind = shift(half, axis, 1), shift(half, axis, -1)
    low = shift(ahead[:rows], axis, 1)
    high = shift(behind[rows:], axis, -1)
    return [(half,), (ahead,), (low, high), (behind,)]


def load(refs, column=slice(None)):
    parts = [ref[:, column] for ref in refs]
    return parts[0] if len(parts) == 1 else jnp.concatenate(parts, axis=0)


def regroup(refs, counts):
    groups = []
    for count in counts:
        groups.append(refs[:count])
        refs = refs[count:]
    return groups


def offsets(sizes):
    return [sum(sizes[:i]) for i in range(len(sizes))]


def in_hbm(*arrays):
    return [pltpu.with_memory_space_constraint(array, pltpu.HBM) for array in arrays]


def prepare_kernel(token_ref, id_ref, gate_ref, a_ref, b_ref):
    tokens, depth = token_ref.shape
    half = depth // 2
    top = id_ref.shape[0]
    given = jnp.concatenate([id_ref[...].astype(jnp.float32), gate_ref[...]], axis=0).T
    lane = lax.broadcasted_iota(jnp.int32, (tokens, TILE), 1)
    number = lane.astype(jnp.float32)
    row = lax.broadcasted_iota(jnp.int32, (tokens, tokens), 0)
    column = lax.broadcasted_iota(jnp.int32, (tokens, tokens), 1)
    ids = [given[:, k : k + 1] for k in range(top)]
    named = jnp.zeros((tokens, TILE), jnp.float32)
    for k in range(top):
        named = jnp.where(ids[k] == number, 1.0, named)
    before = jnp.where(column < row, 1.0, 0.0).astype(jnp.bfloat16)
    rank = jnp.dot(before, named.astype(jnp.bfloat16), preferred_element_type=jnp.float32)
    facts = jnp.zeros((tokens, TILE), jnp.float32)
    for k in range(top):
        place = jnp.sum(jnp.where(ids[k] == number, rank, 0.0), axis=1, keepdims=True)
        facts = jnp.where(lane == k, ids[k], facts)
        facts = jnp.where(lane == top + k, place, facts)
        facts = jnp.where(lane == 2 * top + k, given[:, top + k : top + k + 1], facts)
    facts = facts.astype(jnp.bfloat16)
    a_ref[:, :half] = token_ref[:, :half]
    b_ref[:, :half] = token_ref[:, half:]
    a_ref[:, half:] = facts
    b_ref[:, half:] = facts


def prepare(tokens, expert_ids, gate_values):
    rows, depth = tokens.shape
    out = jax.ShapeDtypeStruct((rows, depth // 2 + TILE), jnp.bfloat16)
    top = expert_ids.shape[1]
    return pl.pallas_call(
        prepare_kernel,
        grid=(1,),
        in_specs=[
            pl.BlockSpec((rows, depth), lambda i: (0, 0)),
            pl.BlockSpec((top, rows), lambda i: (0, 0)),
            pl.BlockSpec((top, rows), lambda i: (0, 0)),
        ],
        out_specs=[pl.BlockSpec(out.shape, lambda i: (0, 0))] * 2,
        out_shape=[out, out],
        compiler_params=pltpu.CompilerParams(vmem_limit_bytes=VMEM),
        cost_estimate=pl.CostEstimate(
            flops=2 * rows * rows * TILE, bytes_accessed=4 * rows * depth, transcendentals=0
        ),
    )(*in_hbm(tokens, expert_ids.T, gate_values.T))


def codes(facts, top):
    facts = facts.astype(jnp.float32)
    return [facts[:, k : k + 1] * CAP + facts[:, top + k : top + k + 1] for k in range(top)]


def targets(experts_ref, pieces, tokens):
    count = sum(rows for _, _, rows in pieces)
    lane = lax.broadcasted_iota(jnp.int32, (tokens, count), 1)
    code = jnp.zeros((tokens, count), jnp.int32)
    low = 0
    for place, first, rows in pieces:
        value = experts_ref[place] * CAP + first + lane - low
        code = jnp.where((lane >= low) & (lane < low + rows), value, code)
        low += rows
    return code.astype(jnp.float32)


def pick_rows(experts_ref, pieces, top, refs, width):
    tokens = sum(ref.shape[0] for ref in refs)
    target = targets(experts_ref, pieces, tokens)
    pick = jnp.zeros(target.shape, jnp.float32)
    for code in codes(load(refs, slice(width, width + TILE)), top):
        pick = jnp.where(code == target, 1.0, pick)
    rows = jnp.dot(
        pick.T.astype(jnp.bfloat16),
        load(refs, slice(0, width)),
        preferred_element_type=jnp.float32,
    )
    return rows.astype(jnp.bfloat16)


def pack_a_kernel(segments, counts, top, experts_ref, *refs):
    *sources, outs = regroup(refs, counts + (SIDE,))
    width = outs[0].shape[-1]
    starts = offsets([rows for _, _, rows in segments])
    for refs, start, (_, first, rows) in zip(sources, starts, segments):
        pieces = [(dest, first, rows) for dest in range(SIDE)]
        picked = pick_rows(experts_ref, pieces, top, refs, width)
        for dest in range(SIDE):
            outs[dest][start : start + rows] = picked[dest * rows : (dest + 1) * rows]


def pack_b_kernel(segments, counts, top, experts_ref, *refs):
    *sources, outs = regroup(refs, counts + (len(segments),))
    width = outs[0].shape[-1]
    starts = offsets([rows for _, _, rows in segments])
    for source, refs in enumerate(sources):
        picked = pick_rows(experts_ref, segments, top, refs, width)
        for out, start, (_, _, rows) in zip(outs, starts, segments):
            out[source * rows : (source + 1) * rows] = picked[start : start + rows]


def pack(kernel, segments, top, experts, sources, sizes):
    tokens, width = sources[0][0].shape
    width -= TILE
    counts = tuple(len(source) for source in sources)
    blocks = [block for source in sources for block in source]
    total = sum(sizes)
    return pl.pallas_call(
        functools.partial(kernel, segments, counts, top),
        in_specs=[pl.BlockSpec(memory_space=pltpu.SMEM)]
        + [pl.BlockSpec(memory_space=pltpu.VMEM)] * len(blocks),
        out_specs=[pl.BlockSpec(memory_space=pltpu.VMEM)] * len(sizes),
        out_shape=[jax.ShapeDtypeStruct((rows, width), jnp.bfloat16) for rows in sizes],
        compiler_params=pltpu.CompilerParams(vmem_limit_bytes=VMEM),
        cost_estimate=pl.CostEstimate(
            flops=2 * total * tokens * width,
            bytes_accessed=2 * width * (tokens * len(sources) + total),
            transcendentals=0,
        ),
    )(experts, *blocks)


def hidden_kernel(segments, wg_ref, wu_ref, *refs):
    a_in, b_in, (hidden_ref, x_ref, sems) = regroup(refs, (SIDE, len(segments), 3))
    half = x_ref.shape[-1] // 2

    @pl.when(pl.program_id(0) == 0)
    def _():
        copies = []

        def move(source, target):
            copies.append(pltpu.make_async_copy(source, target, sems.at[len(copies)]))

        base = start = 0
        for ref, (_, _, rows) in zip(b_in, segments):
            move(ref, x_ref.at[base : base + SIDE * rows, half:])
            for k in range(SIDE):
                low = base + k * rows
                move(a_in[k].at[start : start + rows], x_ref.at[low : low + rows, :half])
            base += SIDE * rows
            start += rows
        for copy in copies:
            copy.start()
        for copy in copies:
            copy.wait()

    x = x_ref[...]
    gate = jnp.dot(x, wg_ref[...], preferred_element_type=jnp.float32)
    up = jnp.dot(x, wu_ref[...], preferred_element_type=jnp.float32)
    hidden_ref[...] = (gate / (1.0 + jnp.exp(-gate)) * up).astype(jnp.bfloat16)


def hidden_rows(segments, w_gate, w_up, a_in, b_in):
    depth, ff = w_gate.shape
    count = SIDE * sum(rows for _, _, rows in segments)
    weight = pl.BlockSpec((depth, FF_TILE), lambda i: (0, i))
    return pl.pallas_call(
        functools.partial(hidden_kernel, segments),
        grid=(ff // FF_TILE,),
        in_specs=[weight, weight]
        + [pl.BlockSpec(memory_space=pl.ANY)] * (SIDE + len(segments)),
        out_specs=pl.BlockSpec((count, FF_TILE), lambda i: (0, i)),
        out_shape=jax.ShapeDtypeStruct((count, ff), jnp.bfloat16),
        scratch_shapes=[
            pltpu.VMEM((count, depth), jnp.bfloat16),
            pltpu.SemaphoreType.DMA(((SIDE + 1) * len(segments),)),
        ],
        compiler_params=pltpu.CompilerParams(vmem_limit_bytes=VMEM),
        cost_estimate=pl.CostEstimate(
            flops=4 * count * depth * ff,
            bytes_accessed=4 * depth * ff + 2 * count * depth,
            transcendentals=count * ff,
        ),
    )(w_gate, w_up, *a_in, *b_in)


def down_kernel(segments, n_half, hidden_ref, wd_ref, *refs):
    a_out, b_out = refs[:SIDE], refs[SIDE:]
    out = jnp.dot(hidden_ref[...], wd_ref[...], preferred_element_type=jnp.float32)
    out = out.astype(jnp.bfloat16)

    @pl.when(pl.program_id(0) < n_half)
    def _():
        base = start = 0
        for _, _, rows in segments:
            for k in range(SIDE):
                low = base + k * rows
                a_out[k][start : start + rows] = out[low : low + rows]
            base += SIDE * rows
            start += rows

    @pl.when(pl.program_id(0) >= n_half)
    def _():
        base = 0
        for ref, (_, _, rows) in zip(b_out, segments):
            ref[...] = out[base : base + SIDE * rows]
            base += SIDE * rows


def down_rows(segments, hidden, w_down):
    count, ff = hidden.shape
    half = w_down.shape[1] // 2
    tile = min(D_TILE, half)
    n_half = half // tile
    sizes = [count // SIDE] * SIDE, [SIDE * rows for _, _, rows in segments]
    a_specs = [
        pl.BlockSpec((rows, tile), lambda i: (0, jnp.minimum(i, n_half - 1)))
        for rows in sizes[0]
    ]
    b_specs = [
        pl.BlockSpec((rows, tile), lambda i: (0, jnp.maximum(i - n_half, 0)))
        for rows in sizes[1]
    ]
    done = pl.pallas_call(
        functools.partial(down_kernel, segments, n_half),
        grid=(2 * n_half,),
        in_specs=[
            pl.BlockSpec((count, ff), lambda i: (0, 0)),
            pl.BlockSpec((ff, tile), lambda i: (0, i)),
        ],
        out_specs=a_specs + b_specs,
        out_shape=[
            jax.ShapeDtypeStruct((rows, half), jnp.bfloat16) for rows in sizes[0] + sizes[1]
        ],
        compiler_params=pltpu.CompilerParams(vmem_limit_bytes=VMEM),
        cost_estimate=pl.CostEstimate(
            flops=4 * count * half * ff,
            bytes_accessed=4 * half * ff + 4 * count * half,
            transcendentals=0,
        ),
    )(hidden, w_down)
    return done[:SIDE], done[SIDE:]


def sum_kernel(top, counts, experts_ref, *refs):
    *groups, a_out, b_out = regroup(refs, counts)
    a_in, b_in = groups[: len(PLAN)], groups[len(PLAN) : 2 * len(PLAN)]
    facts = groups[2 * len(PLAN) :]
    tokens = a_out[0].shape[0]

    def total(refs, pieces, rows, out):
        about = load(refs).astype(jnp.float32)
        target = targets(experts_ref, pieces, tokens)
        weight = jnp.zeros(target.shape, jnp.float32)
        for k, code in enumerate(codes(about, top)):
            gate = about[:, 2 * top + k : 2 * top + k + 1]
            weight = jnp.where(code == target, gate, weight)
        mixed = jnp.dot(
            weight.astype(jnp.bfloat16),
            jnp.concatenate(rows, axis=0),
            preferred_element_type=jnp.float32,
        )
        out[...] = mixed.astype(jnp.bfloat16)

    for source in range(SIDE):
        pieces, parts = [], []
        for ins, segments in zip(a_in, PLAN):
            starts = offsets([rows for _, _, rows in segments])
            for start, (distance, first, rows) in zip(starts, segments):
                if distance == source:
                    pieces += [(dest, first, rows) for dest in range(SIDE)]
                    parts += [ref[start : start + rows] for ref in ins]
        total(facts[source], pieces, parts, a_out[source])
    for source in range(SIDE):
        pieces, parts = [], []
        for ins, segments in zip(b_in, PLAN):
            for ref, (distance, first, rows) in zip(ins, segments):
                pieces.append((SIDE + distance, first, rows))
                parts.append(ref[source * rows : (source + 1) * rows])
        total(facts[SIDE + source], pieces, parts, b_out[source])


def sum_rows(top, experts, a_rows, b_rows, a_back, b_back):
    width = a_back[0][0].shape[-1]
    tokens = a_rows[0][0].shape[0]
    lines = [*a_rows, *b_rows]
    facts = [block for line in lines for block in line]
    last = width // TILE
    whole = pl.BlockSpec(memory_space=pltpu.VMEM)
    out = jax.ShapeDtypeStruct((tokens, width), jnp.bfloat16)
    groups = [*a_back, *b_back]
    blocks = [block for group in groups for block in group]
    counts = tuple(len(group) for group in groups + lines) + (SIDE, SIDE)
    done = pl.pallas_call(
        functools.partial(sum_kernel, top, counts),
        grid=(1,),
        in_specs=[pl.BlockSpec(memory_space=pltpu.SMEM)]
        + [whole] * len(blocks)
        + [pl.BlockSpec((f.shape[0], TILE), lambda i: (0, last)) for f in facts],
        out_specs=[whole] * (2 * SIDE),
        out_shape=[out] * (2 * SIDE),
        compiler_params=pltpu.CompilerParams(vmem_limit_bytes=VMEM),
        cost_estimate=pl.CostEstimate(
            flops=4 * SIDE * SIDE * CAP * tokens * width,
            bytes_accessed=4 * SIDE * width * (tokens + SIDE * CAP),
            transcendentals=0,
        ),
    )(experts, *blocks, *facts)
    return done[:SIDE], done[SIDE:]


def send(segments, a_blocks, b_blocks, a_axis, b_axis, sign):
    a_moved, b_moved = list(a_blocks), list(b_blocks)
    for k in range(1, SIDE):
        a_moved[k] = shift(a_blocks[k], a_axis, sign * k)
    for i, (distance, _, _) in enumerate(segments):
        if distance:
            b_moved[i] = shift(b_blocks[i], b_axis, sign * distance)
    return a_moved, b_moved


def local(tokens, expert_ids, gate_values, gate_weight, up_weight, down_weight):
    top = expert_ids.shape[1]
    z, x = lax.axis_index("z"), lax.axis_index("x")
    steps = jnp.arange(SIDE, dtype=jnp.int32)
    a_experts = z * SIDE + (x + steps) % SIDE
    b_experts = (z + steps) % SIDE * SIDE + x

    a_half, b_half = prepare(tokens, expert_ids, gate_values)
    b_rows = gather_line(b_half, "x")
    a_rows = gather_line(a_half, "z")

    w_gate, w_up, w_down = in_hbm(gate_weight[0], up_weight[0], down_weight[0])
    experts = jnp.concatenate([a_experts, b_experts])
    a_back, b_back, hidden = [], [], None

    def back(segments, hidden):
        a_done, b_done = down_rows(segments, hidden, w_down)
        a_home, b_home = send(segments, a_done, b_done, "x", "z", -1)
        a_back.append(a_home)
        b_back.append(b_home)

    packed = []
    for segments in PLAN:
        rows = [size for _, _, size in segments]
        sources = [a_rows[distance] for distance, _, _ in segments]
        a_out = list(
            pack(pack_a_kernel, segments, top, experts[:SIDE], sources, [sum(rows)] * SIDE)
        )
        sizes = [SIDE * size for size in rows]
        b_out = list(pack(pack_b_kernel, segments, top, experts[SIDE:], b_rows, sizes))
        experts, a_out, b_out = lax.optimization_barrier((experts, a_out, b_out))
        packed.append((a_out, b_out))

    a_in, b_in = send(PLAN[0], *packed[0], "x", "z", 1)
    a_out, b_out = packed[1]
    hidden = hidden_rows(PLAN[0], w_gate, w_up, a_in, b_in)
    b_out[2], hidden = lax.optimization_barrier((b_out[2], hidden))
    back(PLAN[0], hidden)
    a_in, b_in = send(PLAN[1], a_out, b_out, "x", "z", 1)
    hidden = hidden_rows(PLAN[1], w_gate, w_up, a_in, b_in)
    b_back[0][1], b_back[0][2], hidden = lax.optimization_barrier(
        (b_back[0][1], b_back[0][2], hidden)
    )
    back(PLAN[-1], hidden)

    a_sums, b_sums = sum_rows(top, experts, a_rows, b_rows, a_back, b_back)
    line = tuple((distance, 0, 0) for distance in range(SIDE))
    a_home, b_home = send(line, a_sums, b_sums, "z", "x", -1)
    mixed = [sum(part.astype(jnp.float32) for part in home) for home in (a_home, b_home)]
    return jnp.concatenate(mixed, axis=1).astype(jnp.bfloat16)


def solution(mesh):
    dp = mesh.devices.shape[0]
    grid = Mesh(mesh.devices.reshape(dp, SIDE, SIDE), ("dp", "z", "x"))
    rows, experts = ("dp", "z", "x"), ("z", "x")
    in_specs = (
        P(rows, None),
        P(rows, None),
        P(rows, None),
        P(experts, None, None),
        P(experts, None, None),
        P(experts, None, None),
    )
    return jax.shard_map(
        local, mesh=grid, in_specs=in_specs, out_specs=P(rows, None), check_vma=False
    )
```

```python
import functools

import jax
import jax.numpy as jnp
from jax import lax
from jax.experimental import pallas as pl
from jax.experimental.pallas import tpu as pltpu
from jax.sharding import Mesh, PartitionSpec as P

SIDE = 4
CAP = 64
CHUNKS = 2
ROWS = CAP // CHUNKS
TILE = 128
FF_TILE = 256
D_TILE = 1024
VMEM = 36 * 1024 * 1024


def shift(block, axis, step):
    return lax.ppermute(block, axis, [(i, (i + step) % SIDE) for i in range(SIDE)])


def gather_line(half, axis):
    rows = half.shape[0] // 2
    ahead, behind = shift(half, axis, 1), shift(half, axis, -1)
    low = shift(ahead[:rows], axis, 1)
    high = shift(behind[rows:], axis, -1)
    return [half, ahead, low, high, behind]


def line_rows(refs, column=slice(None)):
    own, ahead, low, high, behind = [ref[:, column] for ref in refs]
    return [own, ahead, jnp.concatenate([low, high], axis=0), behind]


def both_ways(a_blocks, b_blocks, a_axis, b_axis, sign):
    a_moved, b_moved = list(a_blocks), list(b_blocks)
    for k in (1, 3, 2):
        a_moved[k] = shift(a_blocks[k], a_axis, sign * k)
        b_moved[k] = shift(b_blocks[k], b_axis, sign * k)
    return a_moved, b_moved


def in_hbm(*arrays):
    return [pltpu.with_memory_space_constraint(array, pltpu.HBM) for array in arrays]


def prepare_kernel(token_ref, id_ref, gate_ref, a_ref, b_ref):
    tokens, depth = token_ref.shape
    half = depth // 2
    top = id_ref.shape[0]
    given = jnp.concatenate([id_ref[...].astype(jnp.float32), gate_ref[...]], axis=0).T
    lane = lax.broadcasted_iota(jnp.int32, (tokens, TILE), 1)
    number = lane.astype(jnp.float32)
    row = lax.broadcasted_iota(jnp.int32, (tokens, tokens), 0)
    column = lax.broadcasted_iota(jnp.int32, (tokens, tokens), 1)
    ids = [given[:, k : k + 1] for k in range(top)]
    named = jnp.zeros((tokens, TILE), jnp.float32)
    for k in range(top):
        named = jnp.where(ids[k] == number, 1.0, named)
    before = jnp.where(column < row, 1.0, 0.0).astype(jnp.bfloat16)
    rank = jnp.dot(before, named.astype(jnp.bfloat16), preferred_element_type=jnp.float32)
    facts = jnp.zeros((tokens, TILE), jnp.float32)
    for k in range(top):
        place = jnp.sum(jnp.where(ids[k] == number, rank, 0.0), axis=1, keepdims=True)
        facts = jnp.where(lane == k, ids[k], facts)
        facts = jnp.where(lane == top + k, place, facts)
        facts = jnp.where(lane == 2 * top + k, given[:, top + k : top + k + 1], facts)
    facts = facts.astype(jnp.bfloat16)
    a_ref[:, :half] = token_ref[:, :half]
    b_ref[:, :half] = token_ref[:, half:]
    a_ref[:, half:] = facts
    b_ref[:, half:] = facts


def prepare(tokens, expert_ids, gate_values):
    rows, depth = tokens.shape
    out = jax.ShapeDtypeStruct((rows, depth // 2 + TILE), jnp.bfloat16)
    top = expert_ids.shape[1]
    return pl.pallas_call(
        prepare_kernel,
        grid=(1,),
        in_specs=[
            pl.BlockSpec((rows, depth), lambda i: (0, 0)),
            pl.BlockSpec((top, rows), lambda i: (0, 0)),
            pl.BlockSpec((top, rows), lambda i: (0, 0)),
        ],
        out_specs=[pl.BlockSpec(out.shape, lambda i: (0, 0))] * 2,
        out_shape=[out, out],
        compiler_params=pltpu.CompilerParams(vmem_limit_bytes=VMEM),
        cost_estimate=pl.CostEstimate(
            flops=2 * rows * rows * TILE, bytes_accessed=4 * rows * depth, transcendentals=0
        ),
    )(*in_hbm(tokens, expert_ids.T, gate_values.T))


def codes(facts, top):
    facts = facts.astype(jnp.float32)
    return [facts[:, k : k + 1] * CAP + facts[:, top + k : top + k + 1] for k in range(top)]


def targets(experts_ref, first, chunks, tokens):
    count = len(chunks) * SIDE * ROWS
    lane = lax.broadcasted_iota(jnp.int32, (tokens, count), 1)
    code = jnp.zeros((tokens, count), jnp.int32)
    for n, chunk in enumerate(chunks):
        for dest in range(SIDE):
            low = (n * SIDE + dest) * ROWS
            value = experts_ref[first + dest] * CAP + chunk * ROWS + lane - low
            code = jnp.where((lane >= low) & (lane < low + ROWS), value, code)
    return code.astype(jnp.float32)


def pack_kernel(chunk, top, experts_ref, *refs):
    blocks, outs = refs[:-SIDE], refs[-SIDE:]
    tokens = blocks[0].shape[0]
    width = outs[0].shape[-1]
    target = targets(experts_ref, 0, (chunk,), tokens)
    facts = line_rows(blocks, slice(width, width + TILE))
    rows_in = line_rows(blocks, slice(0, width))
    for source in range(SIDE):
        pick = jnp.zeros(target.shape, jnp.float32)
        for code in codes(facts[source], top):
            pick = jnp.where(code == target, 1.0, pick)
        rows = jnp.dot(
            pick.T.astype(jnp.bfloat16), rows_in[source], preferred_element_type=jnp.float32
        ).astype(jnp.bfloat16)
        for dest in range(SIDE):
            outs[dest][source] = rows[dest * ROWS : (dest + 1) * ROWS]


def pack(chunk, top, experts, blocks):
    tokens, width = blocks[0].shape
    width -= TILE
    out = jax.ShapeDtypeStruct((SIDE, ROWS, width), jnp.bfloat16)
    return pl.pallas_call(
        functools.partial(pack_kernel, chunk, top),
        in_specs=[pl.BlockSpec(memory_space=pltpu.SMEM)]
        + [pl.BlockSpec(memory_space=pltpu.VMEM)] * len(blocks),
        out_specs=[pl.BlockSpec(memory_space=pltpu.VMEM)] * SIDE,
        out_shape=[out] * SIDE,
        compiler_params=pltpu.CompilerParams(vmem_limit_bytes=VMEM),
        cost_estimate=pl.CostEstimate(
            flops=2 * SIDE * SIDE * ROWS * tokens * width,
            bytes_accessed=2 * SIDE * width * (tokens + SIDE * ROWS),
            transcendentals=0,
        ),
    )(experts, *blocks)


def hidden_kernel(wg_ref, wu_ref, *refs):
    a_in, b_in = refs[:SIDE], refs[SIDE : 2 * SIDE]
    hidden_ref, x_ref, sems = refs[2 * SIDE :]
    half = x_ref.shape[-1] // 2
    count = SIDE * SIDE * ROWS

    @pl.when(pl.program_id(0) == 0)
    def _():
        copies = []
        for k in range(SIDE):
            copies.append(
                pltpu.make_async_copy(a_in[k], x_ref.at[:, k, :, :half], sems.at[k])
            )
            copies.append(
                pltpu.make_async_copy(b_in[k], x_ref.at[k, :, :, half:], sems.at[SIDE + k])
            )
        for copy in copies:
            copy.start()
        for copy in copies:
            copy.wait()

    x = x_ref[...].reshape(count, 2 * half)
    gate = jnp.dot(x, wg_ref[...], preferred_element_type=jnp.float32)
    up = jnp.dot(x, wu_ref[...], preferred_element_type=jnp.float32)
    hidden_ref[...] = (gate / (1.0 + jnp.exp(-gate)) * up).astype(jnp.bfloat16)


def hidden_rows(w_gate, w_up, a_in, b_in):
    depth, ff = w_gate.shape
    count = SIDE * SIDE * ROWS
    weight = pl.BlockSpec((depth, FF_TILE), lambda i: (0, i))
    return pl.pallas_call(
        hidden_kernel,
        grid=(ff // FF_TILE,),
        in_specs=[weight, weight] + [pl.BlockSpec(memory_space=pl.ANY)] * (2 * SIDE),
        out_specs=pl.BlockSpec((count, FF_TILE), lambda i: (0, i)),
        out_shape=jax.ShapeDtypeStruct((count, ff), jnp.bfloat16),
        scratch_shapes=[
            pltpu.VMEM((SIDE, SIDE, ROWS, depth), jnp.bfloat16),
            pltpu.SemaphoreType.DMA((2 * SIDE,)),
        ],
        compiler_params=pltpu.CompilerParams(vmem_limit_bytes=VMEM),
        cost_estimate=pl.CostEstimate(
            flops=4 * count * depth * ff,
            bytes_accessed=4 * depth * ff + 2 * count * depth,
            transcendentals=count * ff,
        ),
    )(w_gate, w_up, *a_in, *b_in)


def down_kernel(n_half, hidden_ref, wd_ref, *refs):
    a_out, b_out = refs[:SIDE], refs[SIDE:]
    out = jnp.dot(hidden_ref[...], wd_ref[...], preferred_element_type=jnp.float32)
    out = out.astype(jnp.bfloat16).reshape(SIDE, SIDE, ROWS, out.shape[1])

    @pl.when(pl.program_id(0) < n_half)
    def _():
        for k in range(SIDE):
            a_out[k][...] = out[:, k]

    @pl.when(pl.program_id(0) >= n_half)
    def _():
        for k in range(SIDE):
            b_out[k][...] = out[k]


def down_rows(hidden, w_down):
    count, ff = hidden.shape
    half = w_down.shape[1] // 2
    tile = min(D_TILE, half)
    n_half = half // tile
    a_spec = pl.BlockSpec((SIDE, ROWS, tile), lambda i: (0, 0, jnp.minimum(i, n_half - 1)))
    b_spec = pl.BlockSpec((SIDE, ROWS, tile), lambda i: (0, 0, jnp.maximum(i - n_half, 0)))
    out = jax.ShapeDtypeStruct((SIDE, ROWS, half), jnp.bfloat16)
    done = pl.pallas_call(
        functools.partial(down_kernel, n_half),
        grid=(2 * n_half,),
        in_specs=[
            pl.BlockSpec((count, ff), lambda i: (0, 0)),
            pl.BlockSpec((ff, tile), lambda i: (0, i)),
        ],
        out_specs=[a_spec] * SIDE + [b_spec] * SIDE,
        out_shape=[out] * (2 * SIDE),
        compiler_params=pltpu.CompilerParams(vmem_limit_bytes=VMEM),
        cost_estimate=pl.CostEstimate(
            flops=4 * count * half * ff,
            bytes_accessed=4 * half * ff + 4 * count * half,
            transcendentals=0,
        ),
    )(hidden, w_down)
    return done[:SIDE], done[SIDE:]


def sum_kernel(top, counts, experts_ref, *refs):
    groups = []
    for count in counts:
        groups.append(refs[:count])
        refs = refs[count:]
    a_in, b_in, a_facts, b_facts, a_out, b_out = groups
    tokens = a_out[0].shape[0]
    for first, ins, blocks, outs in ((0, a_in, a_facts, a_out), (SIDE, b_in, b_facts, b_out)):
        target = targets(experts_ref, first, tuple(range(CHUNKS)), tokens)
        facts = line_rows(blocks)
        for source in range(SIDE):
            wide = facts[source].astype(jnp.float32)
            weight = jnp.zeros(target.shape, jnp.float32)
            for k, code in enumerate(codes(wide, top)):
                gate = wide[:, 2 * top + k : 2 * top + k + 1]
                weight = jnp.where(code == target, gate, weight)
            rows = jnp.concatenate([ref[source] for ref in ins], axis=0)
            total = jnp.dot(
                weight.astype(jnp.bfloat16), rows, preferred_element_type=jnp.float32
            )
            if first:
                outs[0][experts_ref[2 * SIDE + source]] = total.astype(jnp.bfloat16)
            else:
                outs[source][...] = total.astype(jnp.bfloat16)


def sum_rows(top, experts, a_facts, b_facts, a_blocks, b_blocks):
    width = a_blocks[0].shape[-1]
    tokens = a_facts[0].shape[0]
    facts = [*a_facts, *b_facts]
    last = width // TILE
    whole = pl.BlockSpec(memory_space=pltpu.VMEM)
    out = pltpu.HBM((tokens, width), jnp.bfloat16)
    counts = (len(a_blocks), len(b_blocks), len(a_facts), len(b_facts), SIDE, 1)
    line = pltpu.HBM((SIDE, tokens, width), jnp.bfloat16)
    done = pl.pallas_call(
        functools.partial(sum_kernel, top, counts),
        grid=(1,),
        in_specs=[pl.BlockSpec(memory_space=pltpu.SMEM)]
        + [whole] * (len(a_blocks) + len(b_blocks))
        + [pl.BlockSpec((f.shape[0], TILE), lambda i: (0, last)) for f in facts],
        out_specs=[pl.BlockSpec(out.shape, lambda i: (0, 0))] * SIDE
        + [pl.BlockSpec(line.shape, lambda i: (0, 0, 0))],
        out_shape=[out] * SIDE + [line],
        compiler_params=pltpu.CompilerParams(vmem_limit_bytes=VMEM),
        cost_estimate=pl.CostEstimate(
            flops=4 * SIDE * SIDE * CAP * tokens * width,
            bytes_accessed=4 * SIDE * width * (tokens + SIDE * CAP),
            transcendentals=0,
        ),
    )(experts, *a_blocks, *b_blocks, *facts)
    return done[:SIDE], done[SIDE]


def local(tokens, expert_ids, gate_values, gate_weight, up_weight, down_weight):
    top = expert_ids.shape[1]
    z, x = lax.axis_index("z"), lax.axis_index("x")
    steps = jnp.arange(SIDE, dtype=jnp.int32)
    a_experts = z * SIDE + (x + steps) % SIDE
    b_experts = (z + steps) % SIDE * SIDE + x

    a_half, b_half = prepare(tokens, expert_ids, gate_values)
    b_rows = gather_line(b_half, "x")
    a_rows = gather_line(a_half, "z")

    w_gate, w_up, w_down = in_hbm(gate_weight[0], up_weight[0], down_weight[0])
    a_back, b_back = [], []
    for chunk in range(CHUNKS):
        a_out = list(pack(chunk, top, a_experts, a_rows))
        b_out = list(pack(chunk, top, b_experts, b_rows))
        a_experts, b_experts, a_out, b_out = lax.optimization_barrier(
            (a_experts, b_experts, a_out, b_out)
        )
        if chunk:
            b_out[2], hidden = lax.optimization_barrier((b_out[2], hidden))
            a_done, b_done = down_rows(hidden, w_down)
            a_home, b_home = both_ways(a_done, b_done, "x", "z", -1)
            a_back += a_home
            b_back += b_home
        a_in, b_in = both_ways(a_out, b_out, "x", "z", 1)
        hidden = hidden_rows(w_gate, w_up, a_in, b_in)
    hidden, a_back[1] = lax.optimization_barrier((hidden, a_back[1]))
    a_done, b_done = down_rows(hidden, w_down)
    a_home, b_home = both_ways(a_done, b_done, "x", "z", -1)
    a_back += a_home
    b_back += b_home

    experts = jnp.concatenate([a_experts, b_experts, (x - steps) % SIDE])
    a_sums, b_sums = sum_rows(top, experts, a_rows, b_rows, a_back, b_back)
    b_home = lax.all_to_all(b_sums, "x", 0, 0, tiled=True)
    a_home = [a_sums[0]] + [shift(a_sums[k], "z", -k) for k in range(1, SIDE)]
    a_mixed = sum(part.astype(jnp.float32) for part in a_home)
    b_mixed = jnp.sum(b_home.astype(jnp.float32), axis=0)
    return jnp.concatenate([a_mixed, b_mixed], axis=1).astype(jnp.bfloat16)


def solution(mesh):
    dp = mesh.devices.shape[0]
    grid = Mesh(mesh.devices.reshape(dp, SIDE, SIDE), ("dp", "z", "x"))
    rows, experts = ("dp", "z", "x"), ("z", "x")
    in_specs = (
        P(rows, None),
        P(rows, None),
        P(rows, None),
        P(experts, None, None),
        P(experts, None, None),
        P(experts, None, None),
    )
    return jax.shard_map(
        local, mesh=grid, in_specs=in_specs, out_specs=P(rows, None), check_vma=False
    )
```

```python
import functools

import jax
import jax.numpy as jnp
from jax import lax
from jax.experimental import pallas as pl
from jax.experimental.pallas import tpu as pltpu
from jax.sharding import Mesh, PartitionSpec as P

SIDE = 4
CAP = 64
NEAR = tuple((i, k) for i in range(SIDE) for k in range(SIDE) if 2 not in (i, k))
FAR = tuple((i, k) for i in range(SIDE) for k in range(SIDE) if 2 in (i, k))
PLAN = (NEAR, FAR)
TILE = 128
FF_TILE = 256
D_TILE = 1024
VMEM = 36 * 1024 * 1024


def shift(block, axis, step):
    return lax.ppermute(block, axis, [(i, (i + step) % SIDE) for i in range(SIDE)])


def gather_line(half, axis):
    rows = half.shape[0] // 2
    ahead, behind = shift(half, axis, 1), shift(half, axis, -1)
    low = shift(ahead[:rows], axis, 1)
    high = shift(behind[rows:], axis, -1)
    return [(half,), (ahead,), (low, high), (behind,)]


def load(refs, column=slice(None)):
    parts = [ref[:, column] for ref in refs]
    return parts[0] if len(parts) == 1 else jnp.concatenate(parts, axis=0)


def regroup(refs, counts):
    groups = []
    for count in counts:
        groups.append(refs[:count])
        refs = refs[count:]
    return groups


def line_blocks(blocks, axis):
    lines = {}
    for number, block in enumerate(blocks):
        lines.setdefault(block[axis], []).append(number)
    return dict(sorted(lines.items()))


def in_hbm(*arrays):
    return [pltpu.with_memory_space_constraint(array, pltpu.HBM) for array in arrays]


def prepare_kernel(token_ref, id_ref, gate_ref, a_ref, b_ref):
    tokens, depth = token_ref.shape
    half = depth // 2
    top = id_ref.shape[0]
    given = jnp.concatenate([id_ref[...].astype(jnp.float32), gate_ref[...]], axis=0).T
    lane = lax.broadcasted_iota(jnp.int32, (tokens, TILE), 1)
    number = lane.astype(jnp.float32)
    row = lax.broadcasted_iota(jnp.int32, (tokens, tokens), 0)
    column = lax.broadcasted_iota(jnp.int32, (tokens, tokens), 1)
    ids = [given[:, k : k + 1] for k in range(top)]
    named = jnp.zeros((tokens, TILE), jnp.float32)
    for k in range(top):
        named = jnp.where(ids[k] == number, 1.0, named)
    before = jnp.where(column < row, 1.0, 0.0).astype(jnp.bfloat16)
    rank = jnp.dot(before, named.astype(jnp.bfloat16), preferred_element_type=jnp.float32)
    facts = jnp.zeros((tokens, TILE), jnp.float32)
    for k in range(top):
        place = jnp.sum(jnp.where(ids[k] == number, rank, 0.0), axis=1, keepdims=True)
        facts = jnp.where(lane == k, ids[k], facts)
        facts = jnp.where(lane == top + k, place, facts)
        facts = jnp.where(lane == 2 * top + k, given[:, top + k : top + k + 1], facts)
    facts = facts.astype(jnp.bfloat16)
    a_ref[:, :half] = token_ref[:, :half]
    b_ref[:, :half] = token_ref[:, half:]
    a_ref[:, half:] = facts
    b_ref[:, half:] = facts


def prepare(tokens, expert_ids, gate_values):
    rows, depth = tokens.shape
    out = jax.ShapeDtypeStruct((rows, depth // 2 + TILE), jnp.bfloat16)
    top = expert_ids.shape[1]
    return pl.pallas_call(
        prepare_kernel,
        grid=(1,),
        in_specs=[
            pl.BlockSpec((rows, depth), lambda i: (0, 0)),
            pl.BlockSpec((top, rows), lambda i: (0, 0)),
            pl.BlockSpec((top, rows), lambda i: (0, 0)),
        ],
        out_specs=[pl.BlockSpec(out.shape, lambda i: (0, 0))] * 2,
        out_shape=[out, out],
        compiler_params=pltpu.CompilerParams(vmem_limit_bytes=VMEM),
        cost_estimate=pl.CostEstimate(
            flops=2 * rows * rows * TILE, bytes_accessed=4 * rows * depth, transcendentals=0
        ),
    )(*in_hbm(tokens, expert_ids.T, gate_values.T))


def codes(facts, top):
    facts = facts.astype(jnp.float32)
    return [facts[:, k : k + 1] * CAP + facts[:, top + k : top + k + 1] for k in range(top)]


def targets(experts_ref, places, tokens):
    count = len(places) * CAP
    lane = lax.broadcasted_iota(jnp.int32, (tokens, count), 1)
    code = jnp.zeros((tokens, count), jnp.int32)
    for i, place in enumerate(places):
        low = i * CAP
        value = experts_ref[place] * CAP + lane - low
        code = jnp.where((lane >= low) & (lane < low + CAP), value, code)
    return code.astype(jnp.float32)


def pick_rows(experts_ref, places, top, refs, width):
    tokens = sum(ref.shape[0] for ref in refs)
    target = targets(experts_ref, places, tokens)
    pick = jnp.zeros(target.shape, jnp.float32)
    for code in codes(load(refs, slice(width, width + TILE)), top):
        pick = jnp.where(code == target, 1.0, pick)
    rows = jnp.dot(
        pick.T.astype(jnp.bfloat16),
        load(refs, slice(0, width)),
        preferred_element_type=jnp.float32,
    )
    return rows.astype(jnp.bfloat16)


def pack_kernel(blocks, axis, counts, top, experts_ref, *refs):
    sources, targets_to = line_blocks(blocks, axis), line_blocks(blocks, 1 - axis)
    *lines, outs = regroup(refs, counts + (len(targets_to),))
    outs = dict(zip(targets_to, outs))
    width = next(iter(outs.values())).shape[-1]
    for refs, numbers in zip(lines, sources.values()):
        to = [blocks[number][1 - axis] for number in numbers]
        places = [axis * SIDE + distance for distance in to]
        picked = pick_rows(experts_ref, places, top, refs, width)
        for i, (distance, number) in enumerate(zip(to, numbers)):
            low = targets_to[distance].index(number) * CAP
            outs[distance][low : low + CAP] = picked[i * CAP : (i + 1) * CAP]


def pack(blocks, axis, top, experts, lines):
    sources, targets_to = line_blocks(blocks, axis), line_blocks(blocks, 1 - axis)
    lines = [lines[distance] for distance in sources]
    tokens, width = lines[0][0].shape
    width -= TILE
    counts = tuple(len(line) for line in lines)
    arrays = [array for line in lines for array in line]
    sizes = [len(numbers) * CAP for numbers in targets_to.values()]
    done = pl.pallas_call(
        functools.partial(pack_kernel, blocks, axis, counts, top),
        in_specs=[pl.BlockSpec(memory_space=pltpu.SMEM)]
        + [pl.BlockSpec(memory_space=pltpu.VMEM)] * len(arrays),
        out_specs=[pl.BlockSpec(memory_space=pltpu.VMEM)] * len(sizes),
        out_shape=[jax.ShapeDtypeStruct((rows, width), jnp.bfloat16) for rows in sizes],
        compiler_params=pltpu.CompilerParams(vmem_limit_bytes=VMEM),
        cost_estimate=pl.CostEstimate(
            flops=2 * sum(sizes) * tokens * width,
            bytes_accessed=2 * width * (tokens * len(lines) + sum(sizes)),
            transcendentals=0,
        ),
    )(experts, *arrays)
    return dict(zip(targets_to, done))


def hidden_kernel(blocks, wg_ref, wu_ref, *refs):
    by_z, by_x = line_blocks(blocks, 0), line_blocks(blocks, 1)
    a_in, b_in, (hidden_ref, x_ref, sems) = regroup(refs, (len(by_x), len(by_z), 3))
    half = x_ref.shape[-1] // 2

    @pl.when(pl.program_id(0) == 0)
    def _():
        copies = []

        def move(source, target):
            copies.append(pltpu.make_async_copy(source, target, sems.at[len(copies)]))

        for ref, numbers in zip(b_in, by_z.values()):
            low = numbers[0] * CAP
            move(ref, x_ref.at[low : low + len(numbers) * CAP, half:])
        for ref, numbers in zip(a_in, by_x.values()):
            for i, number in enumerate(numbers):
                low = number * CAP
                move(ref.at[i * CAP : (i + 1) * CAP], x_ref.at[low : low + CAP, :half])
        for copy in copies:
            copy.start()
        for copy in copies:
            copy.wait()

    x = x_ref[...]
    gate = jnp.dot(x, wg_ref[...], preferred_element_type=jnp.float32)
    up = jnp.dot(x, wu_ref[...], preferred_element_type=jnp.float32)
    hidden_ref[...] = (gate / (1.0 + jnp.exp(-gate)) * up).astype(jnp.bfloat16)


def hidden_rows(blocks, w_gate, w_up, a_in, b_in):
    depth, ff = w_gate.shape
    count = len(blocks) * CAP
    weight = pl.BlockSpec((depth, FF_TILE), lambda i: (0, i))
    return pl.pallas_call(
        functools.partial(hidden_kernel, blocks),
        grid=(ff // FF_TILE,),
        in_specs=[weight, weight]
        + [pl.BlockSpec(memory_space=pl.ANY)] * (len(a_in) + len(b_in)),
        out_specs=pl.BlockSpec((count, FF_TILE), lambda i: (0, i)),
        out_shape=jax.ShapeDtypeStruct((count, ff), jnp.bfloat16),
        scratch_shapes=[
            pltpu.VMEM((count, depth), jnp.bfloat16),
            pltpu.SemaphoreType.DMA((len(b_in) + len(blocks),)),
        ],
        compiler_params=pltpu.CompilerParams(vmem_limit_bytes=VMEM),
        cost_estimate=pl.CostEstimate(
            flops=4 * count * depth * ff,
            bytes_accessed=4 * depth * ff + 2 * count * depth,
            transcendentals=count * ff,
        ),
    )(w_gate, w_up, *a_in.values(), *b_in.values())


def down_kernel(blocks, n_half, hidden_ref, wd_ref, *refs):
    by_z, by_x = line_blocks(blocks, 0), line_blocks(blocks, 1)
    a_out, b_out = regroup(refs, (len(by_x), len(by_z)))
    out = jnp.dot(hidden_ref[...], wd_ref[...], preferred_element_type=jnp.float32)
    out = out.astype(jnp.bfloat16)

    def hand(outs, lines):
        for ref, numbers in zip(outs, lines.values()):
            for i, number in enumerate(numbers):
                ref[i * CAP : (i + 1) * CAP] = out[number * CAP : (number + 1) * CAP]

    @pl.when(pl.program_id(0) < n_half)
    def _():
        hand(a_out, by_x)

    @pl.when(pl.program_id(0) >= n_half)
    def _():
        hand(b_out, by_z)


def down_rows(blocks, hidden, w_down):
    by_z, by_x = line_blocks(blocks, 0), line_blocks(blocks, 1)
    count, ff = hidden.shape
    half = w_down.shape[1] // 2
    tile = min(D_TILE, half)
    n_half = half // tile
    a_sizes = [len(numbers) * CAP for numbers in by_x.values()]
    b_sizes = [len(numbers) * CAP for numbers in by_z.values()]
    a_specs = [
        pl.BlockSpec((rows, tile), lambda i: (0, jnp.minimum(i, n_half - 1)))
        for rows in a_sizes
    ]
    b_specs = [
        pl.BlockSpec((rows, tile), lambda i: (0, jnp.maximum(i - n_half, 0)))
        for rows in b_sizes
    ]
    done = pl.pallas_call(
        functools.partial(down_kernel, blocks, n_half),
        grid=(2 * n_half,),
        in_specs=[
            pl.BlockSpec((count, ff), lambda i: (0, 0)),
            pl.BlockSpec((ff, tile), lambda i: (0, i)),
        ],
        out_specs=a_specs + b_specs,
        out_shape=[
            jax.ShapeDtypeStruct((rows, half), jnp.bfloat16) for rows in a_sizes + b_sizes
        ],
        compiler_params=pltpu.CompilerParams(vmem_limit_bytes=VMEM),
        cost_estimate=pl.CostEstimate(
            flops=4 * count * half * ff,
            bytes_accessed=4 * half * ff + 4 * count * half,
            transcendentals=0,
        ),
    )(hidden, w_down)
    return dict(zip(by_x, done[: len(by_x)])), dict(zip(by_z, done[len(by_x) :]))


def sum_kernel(top, counts, experts_ref, *refs):
    *groups, a_out, b_out = regroup(refs, counts)
    facts = groups[-2 * SIDE :]
    tokens = a_out[0].shape[0]

    def total(axis, source):
        about = load(facts[axis * SIDE + source]).astype(jnp.float32)
        places = [axis * SIDE + distance for distance in range(SIDE)]
        target = targets(experts_ref, places, tokens)
        weight = jnp.zeros(target.shape, jnp.float32)
        for k, code in enumerate(codes(about, top)):
            gate = about[:, 2 * top + k : 2 * top + k + 1]
            weight = jnp.where(code == target, gate, weight)
        rows = []
        for distance in range(SIDE):
            block = (source, distance) if axis == 0 else (distance, source)
            chunk = next(c for c, blocks in enumerate(PLAN) if block in blocks)
            lines = line_blocks(PLAN[chunk], 1 - axis)
            low = lines[distance].index(PLAN[chunk].index(block)) * CAP
            ref = groups[axis * len(PLAN) + chunk][list(lines).index(distance)]
            rows.append(ref[low : low + CAP])
        mixed = jnp.dot(
            weight.astype(jnp.bfloat16),
            jnp.concatenate(rows, axis=0),
            preferred_element_type=jnp.float32,
        )
        return mixed.astype(jnp.bfloat16)

    for source in range(SIDE):
        b_out[0][experts_ref[2 * SIDE + source]] = total(1, source)
    for source in range(SIDE):
        a_out[source][...] = total(0, source)


def sum_rows(top, experts, a_rows, b_rows, a_back, b_back):
    width = a_back[0][0].shape[-1]
    tokens = a_rows[0][0].shape[0]
    lines = [*a_rows, *b_rows]
    facts = [array for line in lines for array in line]
    last = width // TILE
    whole = pl.BlockSpec(memory_space=pltpu.VMEM)
    groups = [tuple(chunk.values()) for chunk in a_back + b_back]
    arrays = [array for group in groups for array in group]
    counts = tuple(len(group) for group in groups + lines) + (SIDE, 1)
    out = pltpu.HBM((tokens, width), jnp.bfloat16)
    line = pltpu.HBM((SIDE, tokens, width), jnp.bfloat16)
    done = pl.pallas_call(
        functools.partial(sum_kernel, top, counts),
        grid=(1,),
        in_specs=[pl.BlockSpec(memory_space=pltpu.SMEM)]
        + [whole] * len(arrays)
        + [pl.BlockSpec((f.shape[0], TILE), lambda i: (0, last)) for f in facts],
        out_specs=[pl.BlockSpec(out.shape, lambda i: (0, 0))] * SIDE
        + [pl.BlockSpec(line.shape, lambda i: (0, 0, 0))],
        out_shape=[out] * SIDE + [line],
        compiler_params=pltpu.CompilerParams(vmem_limit_bytes=VMEM),
        cost_estimate=pl.CostEstimate(
            flops=4 * SIDE * SIDE * CAP * tokens * width,
            bytes_accessed=4 * SIDE * width * (tokens + SIDE * CAP),
            transcendentals=0,
        ),
    )(experts, *arrays, *facts)
    return done[:SIDE], done[SIDE]


def send(blocks, axis, sign):
    return {
        distance: shift(block, axis, sign * distance) if distance else block
        for distance, block in blocks.items()
    }


def local(tokens, expert_ids, gate_values, gate_weight, up_weight, down_weight):
    top = expert_ids.shape[1]
    z, x = lax.axis_index("z"), lax.axis_index("x")
    steps = jnp.arange(SIDE, dtype=jnp.int32)
    experts = jnp.concatenate(
        [z * SIDE + (x + steps) % SIDE, (z + steps) % SIDE * SIDE + x, (x - steps) % SIDE]
    )

    a_half, b_half = prepare(tokens, expert_ids, gate_values)
    b_rows = gather_line(b_half, "x")
    a_rows = gather_line(a_half, "z")

    w_gate, w_up, w_down = in_hbm(gate_weight[0], up_weight[0], down_weight[0])
    packed = []
    for blocks in PLAN:
        a_out = pack(blocks, 0, top, experts, a_rows)
        b_out = pack(blocks, 1, top, experts, b_rows)
        experts, a_out, b_out = lax.optimization_barrier((experts, a_out, b_out))
        packed.append((a_out, b_out))

    (a_out, b_out), (a_late, b_late) = packed
    hidden = hidden_rows(NEAR, w_gate, w_up, send(a_out, "x", 1), send(b_out, "z", 1))
    b_late[3], hidden = lax.optimization_barrier((b_late[3], hidden))
    a_done, b_done = down_rows(NEAR, hidden, w_down)
    a_back, b_back = [send(a_done, "x", -1)], [send(b_done, "z", -1)]
    hidden = hidden_rows(FAR, w_gate, w_up, send(a_late, "x", 1), send(b_late, "z", 1))
    a_done, b_done = down_rows(FAR, hidden, w_down)
    a_back.append(send(a_done, "x", -1))
    b_back.append(send(b_done, "z", -1))

    a_sums, b_sums = sum_rows(top, experts, a_rows, b_rows, a_back, b_back)
    b_home = lax.all_to_all(b_sums, "x", 0, 0, tiled=True)
    a_home = [a_sums[0]] + [shift(a_sums[k], "z", -k) for k in range(1, SIDE)]
    a_mixed = sum(part.astype(jnp.float32) for part in a_home)
    b_mixed = jnp.sum(b_home.astype(jnp.float32), axis=0)
    return jnp.concatenate([a_mixed, b_mixed], axis=1).astype(jnp.bfloat16)


def solution(mesh):
    dp = mesh.devices.shape[0]
    grid = Mesh(mesh.devices.reshape(dp, SIDE, SIDE), ("dp", "z", "x"))
    rows, experts = ("dp", "z", "x"), ("z", "x")
    in_specs = (
        P(rows, None),
        P(rows, None),
        P(rows, None),
        P(experts, None, None),
        P(experts, None, None),
        P(experts, None, None),
    )
    return jax.shard_map(
        local, mesh=grid, in_specs=in_specs, out_specs=P(rows, None), check_vma=False
    )
```

```python
import functools

import jax
import jax.numpy as jnp
from jax import lax
from jax.experimental import pallas as pl
from jax.experimental.pallas import tpu as pltpu
from jax.sharding import Mesh, PartitionSpec as P

SIDE = 4
CAP = 64
CHUNKS = 2
ROWS = CAP // CHUNKS
TILE = 128
FF_TILE = 256
D_TILE = 1024
VMEM = 36 * 1024 * 1024


def shift(block, axis, step):
    return lax.ppermute(block, axis, [(i, (i + step) % SIDE) for i in range(SIDE)])


def gather_line(half, axis):
    rows = half.shape[0] // 2
    ahead, behind = shift(half, axis, 1), shift(half, axis, -1)
    low = shift(ahead[:rows], axis, 1)
    high = shift(behind[rows:], axis, -1)
    return [half, ahead, low, high, behind]


def line_rows(refs, column=slice(None)):
    own, ahead, low, high, behind = [ref[:, column] for ref in refs]
    return [own, ahead, jnp.concatenate([low, high], axis=0), behind]


def both_ways(a_blocks, b_blocks, a_axis, b_axis, sign):
    a_moved, b_moved = list(a_blocks), list(b_blocks)
    for k in (1, 3, 2):
        a_moved[k] = shift(a_blocks[k], a_axis, sign * k)
        b_moved[k] = shift(b_blocks[k], b_axis, sign * k)
    return a_moved, b_moved


def in_hbm(*arrays):
    return [pltpu.with_memory_space_constraint(array, pltpu.HBM) for array in arrays]


def prepare_kernel(token_ref, id_ref, gate_ref, a_ref, b_ref):
    tokens, depth = token_ref.shape
    half = depth // 2
    top = id_ref.shape[0]
    given = jnp.concatenate([id_ref[...].astype(jnp.float32), gate_ref[...]], axis=0).T
    lane = lax.broadcasted_iota(jnp.int32, (tokens, TILE), 1)
    number = lane.astype(jnp.float32)
    row = lax.broadcasted_iota(jnp.int32, (tokens, tokens), 0)
    column = lax.broadcasted_iota(jnp.int32, (tokens, tokens), 1)
    ids = [given[:, k : k + 1] for k in range(top)]
    named = jnp.zeros((tokens, TILE), jnp.float32)
    for k in range(top):
        named = jnp.where(ids[k] == number, 1.0, named)
    before = jnp.where(column < row, 1.0, 0.0).astype(jnp.bfloat16)
    rank = jnp.dot(before, named.astype(jnp.bfloat16), preferred_element_type=jnp.float32)
    facts = jnp.zeros((tokens, TILE), jnp.float32)
    for k in range(top):
        place = jnp.sum(jnp.where(ids[k] == number, rank, 0.0), axis=1, keepdims=True)
        facts = jnp.where(lane == k, ids[k], facts)
        facts = jnp.where(lane == top + k, place, facts)
        facts = jnp.where(lane == 2 * top + k, given[:, top + k : top + k + 1], facts)
    facts = facts.astype(jnp.bfloat16)
    a_ref[:, :half] = token_ref[:, :half]
    b_ref[:, :half] = token_ref[:, half:]
    a_ref[:, half:] = facts
    b_ref[:, half:] = facts


def prepare(tokens, expert_ids, gate_values):
    rows, depth = tokens.shape
    out = jax.ShapeDtypeStruct((rows, depth // 2 + TILE), jnp.bfloat16)
    top = expert_ids.shape[1]
    return pl.pallas_call(
        prepare_kernel,
        grid=(1,),
        in_specs=[
            pl.BlockSpec((rows, depth), lambda i: (0, 0)),
            pl.BlockSpec((top, rows), lambda i: (0, 0)),
            pl.BlockSpec((top, rows), lambda i: (0, 0)),
        ],
        out_specs=[pl.BlockSpec(out.shape, lambda i: (0, 0))] * 2,
        out_shape=[out, out],
        compiler_params=pltpu.CompilerParams(vmem_limit_bytes=VMEM),
        cost_estimate=pl.CostEstimate(
            flops=2 * rows * rows * TILE, bytes_accessed=4 * rows * depth, transcendentals=0
        ),
    )(*in_hbm(tokens, expert_ids.T, gate_values.T))


def codes(facts, top):
    facts = facts.astype(jnp.float32)
    return [facts[:, k : k + 1] * CAP + facts[:, top + k : top + k + 1] for k in range(top)]


def targets(experts_ref, first, chunks, tokens):
    count = len(chunks) * SIDE * ROWS
    lane = lax.broadcasted_iota(jnp.int32, (tokens, count), 1)
    code = jnp.zeros((tokens, count), jnp.int32)
    for n, chunk in enumerate(chunks):
        for dest in range(SIDE):
            low = (n * SIDE + dest) * ROWS
            value = experts_ref[first + dest] * CAP + chunk * ROWS + lane - low
            code = jnp.where((lane >= low) & (lane < low + ROWS), value, code)
    return code.astype(jnp.float32)


def pack_kernel(chunk, top, experts_ref, *refs):
    blocks, outs = refs[:-SIDE], refs[-SIDE:]
    tokens = blocks[0].shape[0]
    width = outs[0].shape[-1]
    target = targets(experts_ref, 0, (chunk,), tokens)
    facts = line_rows(blocks, slice(width, width + TILE))
    rows_in = line_rows(blocks, slice(0, width))
    for source in range(SIDE):
        pick = jnp.zeros(target.shape, jnp.float32)
        for code in codes(facts[source], top):
            pick = jnp.where(code == target, 1.0, pick)
        rows = jnp.dot(
            pick.T.astype(jnp.bfloat16), rows_in[source], preferred_element_type=jnp.float32
        ).astype(jnp.bfloat16)
        for dest in range(SIDE):
            outs[dest][source] = rows[dest * ROWS : (dest + 1) * ROWS]


def pack(chunk, top, experts, blocks):
    tokens, width = blocks[0].shape
    width -= TILE
    out = jax.ShapeDtypeStruct((SIDE, ROWS, width), jnp.bfloat16)
    return pl.pallas_call(
        functools.partial(pack_kernel, chunk, top),
        in_specs=[pl.BlockSpec(memory_space=pltpu.SMEM)]
        + [pl.BlockSpec(memory_space=pltpu.VMEM)] * len(blocks),
        out_specs=[pl.BlockSpec(memory_space=pltpu.VMEM)] * SIDE,
        out_shape=[out] * SIDE,
        compiler_params=pltpu.CompilerParams(vmem_limit_bytes=VMEM),
        cost_estimate=pl.CostEstimate(
            flops=2 * SIDE * SIDE * ROWS * tokens * width,
            bytes_accessed=2 * SIDE * width * (tokens + SIDE * ROWS),
            transcendentals=0,
        ),
    )(experts, *blocks)


def hidden_kernel(wg_ref, wu_ref, *refs):
    a_in, b_in = refs[:SIDE], refs[SIDE : 2 * SIDE]
    hidden_ref, x_ref, sems = refs[2 * SIDE :]
    half = x_ref.shape[-1] // 2
    count = SIDE * SIDE * ROWS

    first = pl.program_id(0) == 0
    a_copies = [
        pltpu.make_async_copy(a_in[k], x_ref.at[:, k, :, :half], sems.at[k])
        for k in range(SIDE)
    ]
    b_copies = [
        pltpu.make_async_copy(b_in[k], x_ref.at[k, :, :, half:], sems.at[SIDE + k])
        for k in range(SIDE)
    ]

    @pl.when(first)
    def _():
        for copy in b_copies + a_copies:
            copy.start()
        for copy in b_copies:
            copy.wait()

    x = x_ref[:, :, :, half:].reshape(count, half)
    gate = jnp.dot(x, wg_ref[half:], preferred_element_type=jnp.float32)
    up = jnp.dot(x, wu_ref[half:], preferred_element_type=jnp.float32)

    @pl.when(first)
    def _():
        for copy in a_copies:
            copy.wait()

    x = x_ref[:, :, :, :half].reshape(count, half)
    gate += jnp.dot(x, wg_ref[:half], preferred_element_type=jnp.float32)
    up += jnp.dot(x, wu_ref[:half], preferred_element_type=jnp.float32)
    hidden_ref[...] = (gate / (1.0 + jnp.exp(-gate)) * up).astype(jnp.bfloat16)


def hidden_rows(w_gate, w_up, a_in, b_in):
    depth, ff = w_gate.shape
    count = SIDE * SIDE * ROWS
    weight = pl.BlockSpec((depth, FF_TILE), lambda i: (0, i))
    return pl.pallas_call(
        hidden_kernel,
        grid=(ff // FF_TILE,),
        in_specs=[weight, weight] + [pl.BlockSpec(memory_space=pl.ANY)] * (2 * SIDE),
        out_specs=pl.BlockSpec((count, FF_TILE), lambda i: (0, i)),
        out_shape=jax.ShapeDtypeStruct((count, ff), jnp.bfloat16),
        scratch_shapes=[
            pltpu.VMEM((SIDE, SIDE, ROWS, depth), jnp.bfloat16),
            pltpu.SemaphoreType.DMA((2 * SIDE,)),
        ],
        compiler_params=pltpu.CompilerParams(vmem_limit_bytes=VMEM),
        cost_estimate=pl.CostEstimate(
            flops=4 * count * depth * ff,
            bytes_accessed=4 * depth * ff + 2 * count * depth,
            transcendentals=count * ff,
        ),
    )(w_gate, w_up, *a_in, *b_in)


def down_kernel(n_half, hidden_ref, wd_ref, *refs):
    a_out, b_out = refs[:SIDE], refs[SIDE:]
    out = jnp.dot(hidden_ref[...], wd_ref[...], preferred_element_type=jnp.float32)
    out = out.astype(jnp.bfloat16).reshape(SIDE, SIDE, ROWS, out.shape[1])

    @pl.when(pl.program_id(0) < n_half)
    def _():
        for k in range(SIDE):
            a_out[k][...] = out[:, k]

    @pl.when(pl.program_id(0) >= n_half)
    def _():
        for k in range(SIDE):
            b_out[k][...] = out[k]


def down_rows(hidden, w_down):
    count, ff = hidden.shape
    half = w_down.shape[1] // 2
    tile = min(D_TILE, half)
    n_half = half // tile
    a_spec = pl.BlockSpec((SIDE, ROWS, tile), lambda i: (0, 0, jnp.minimum(i, n_half - 1)))
    b_spec = pl.BlockSpec((SIDE, ROWS, tile), lambda i: (0, 0, jnp.maximum(i - n_half, 0)))
    out = jax.ShapeDtypeStruct((SIDE, ROWS, half), jnp.bfloat16)
    done = pl.pallas_call(
        functools.partial(down_kernel, n_half),
        grid=(2 * n_half,),
        in_specs=[
            pl.BlockSpec((count, ff), lambda i: (0, 0)),
            pl.BlockSpec((ff, tile), lambda i: (0, i)),
        ],
        out_specs=[a_spec] * SIDE + [b_spec] * SIDE,
        out_shape=[out] * (2 * SIDE),
        compiler_params=pltpu.CompilerParams(vmem_limit_bytes=VMEM),
        cost_estimate=pl.CostEstimate(
            flops=4 * count * half * ff,
            bytes_accessed=4 * half * ff + 4 * count * half,
            transcendentals=0,
        ),
    )(hidden, w_down)
    return done[:SIDE], done[SIDE:]


def sum_kernel(top, counts, experts_ref, *refs):
    groups = []
    for count in counts:
        groups.append(refs[:count])
        refs = refs[count:]
    a_in, b_in, a_facts, b_facts, a_out, b_out = groups
    tokens = a_out[0].shape[0]
    for first, ins, blocks, outs in ((0, a_in, a_facts, a_out), (SIDE, b_in, b_facts, b_out)):
        target = targets(experts_ref, first, tuple(range(CHUNKS)), tokens)
        facts = line_rows(blocks)
        for source in range(SIDE):
            wide = facts[source].astype(jnp.float32)
            weight = jnp.zeros(target.shape, jnp.float32)
            for k, code in enumerate(codes(wide, top)):
                gate = wide[:, 2 * top + k : 2 * top + k + 1]
                weight = jnp.where(code == target, gate, weight)
            rows = jnp.concatenate([ref[source] for ref in ins], axis=0)
            total = jnp.dot(
                weight.astype(jnp.bfloat16), rows, preferred_element_type=jnp.float32
            )
            if first:
                outs[0][experts_ref[2 * SIDE + source]] = total.astype(jnp.bfloat16)
            else:
                outs[source][...] = total.astype(jnp.bfloat16)


def sum_rows(top, experts, a_facts, b_facts, a_blocks, b_blocks):
    width = a_blocks[0].shape[-1]
    tokens = a_facts[0].shape[0]
    facts = [*a_facts, *b_facts]
    last = width // TILE
    whole = pl.BlockSpec(memory_space=pltpu.VMEM)
    out = pltpu.HBM((tokens, width), jnp.bfloat16)
    counts = (len(a_blocks), len(b_blocks), len(a_facts), len(b_facts), SIDE, 1)
    line = pltpu.HBM((SIDE, tokens, width), jnp.bfloat16)
    done = pl.pallas_call(
        functools.partial(sum_kernel, top, counts),
        grid=(1,),
        in_specs=[pl.BlockSpec(memory_space=pltpu.SMEM)]
        + [whole] * (len(a_blocks) + len(b_blocks))
        + [pl.BlockSpec((f.shape[0], TILE), lambda i: (0, last)) for f in facts],
        out_specs=[pl.BlockSpec(out.shape, lambda i: (0, 0))] * SIDE
        + [pl.BlockSpec(line.shape, lambda i: (0, 0, 0))],
        out_shape=[out] * SIDE + [line],
        compiler_params=pltpu.CompilerParams(vmem_limit_bytes=VMEM),
        cost_estimate=pl.CostEstimate(
            flops=4 * SIDE * SIDE * CAP * tokens * width,
            bytes_accessed=4 * SIDE * width * (tokens + SIDE * CAP),
            transcendentals=0,
        ),
    )(experts, *a_blocks, *b_blocks, *facts)
    return done[:SIDE], done[SIDE]


def local(tokens, expert_ids, gate_values, gate_weight, up_weight, down_weight):
    top = expert_ids.shape[1]
    z, x = lax.axis_index("z"), lax.axis_index("x")
    steps = jnp.arange(SIDE, dtype=jnp.int32)
    a_experts = z * SIDE + (x + steps) % SIDE
    b_experts = (z + steps) % SIDE * SIDE + x

    a_half, b_half = prepare(tokens, expert_ids, gate_values)
    b_rows = gather_line(b_half, "x")
    a_rows = gather_line(a_half, "z")

    w_gate, w_up, w_down = in_hbm(gate_weight[0], up_weight[0], down_weight[0])
    a_back, b_back = [], []
    for chunk in range(CHUNKS):
        a_out = list(pack(chunk, top, a_experts, a_rows))
        b_out = list(pack(chunk, top, b_experts, b_rows))
        a_experts, b_experts, a_out, b_out = lax.optimization_barrier(
            (a_experts, b_experts, a_out, b_out)
        )
        if chunk:
            b_out[2], hidden = lax.optimization_barrier((b_out[2], hidden))
            a_done, b_done = down_rows(hidden, w_down)
            a_home, b_home = both_ways(a_done, b_done, "x", "z", -1)
            a_back += a_home
            b_back += b_home
        a_in, b_in = both_ways(a_out, b_out, "x", "z", 1)
        hidden = hidden_rows(w_gate, w_up, a_in, b_in)
    hidden, a_back[1] = lax.optimization_barrier((hidden, a_back[1]))
    a_done, b_done = down_rows(hidden, w_down)
    a_home, b_home = both_ways(a_done, b_done, "x", "z", -1)
    a_back += a_home
    b_back += b_home

    experts = jnp.concatenate([a_experts, b_experts, (x - steps) % SIDE])
    a_sums, b_sums = sum_rows(top, experts, a_rows, b_rows, a_back, b_back)
    b_home = lax.all_to_all(b_sums, "x", 0, 0, tiled=True)
    a_home = [a_sums[0]] + [shift(a_sums[k], "z", -k) for k in range(1, SIDE)]
    a_mixed = sum(part.astype(jnp.float32) for part in a_home)
    b_mixed = jnp.sum(b_home.astype(jnp.float32), axis=0)
    return jnp.concatenate([a_mixed, b_mixed], axis=1).astype(jnp.bfloat16)


def solution(mesh):
    dp = mesh.devices.shape[0]
    grid = Mesh(mesh.devices.reshape(dp, SIDE, SIDE), ("dp", "z", "x"))
    rows, experts = ("dp", "z", "x"), ("z", "x")
    in_specs = (
        P(rows, None),
        P(rows, None),
        P(rows, None),
        P(experts, None, None),
        P(experts, None, None),
        P(experts, None, None),
    )
    return jax.shard_map(
        local, mesh=grid, in_specs=in_specs, out_specs=P(rows, None), check_vma=False
    )
```

```python
import functools

import jax
import jax.numpy as jnp
from jax import lax
from jax.experimental import pallas as pl
from jax.experimental.pallas import tpu as pltpu
from jax.sharding import Mesh, PartitionSpec as P

SIDE = 4
CAP = 64
CHUNKS = 2
ROWS = CAP // CHUNKS
TILE = 128
FF_TILE = 256
D_TILE = 1024
VMEM = 36 * 1024 * 1024


def shift(block, axis, step):
    return lax.ppermute(block, axis, [(i, (i + step) % SIDE) for i in range(SIDE)])


def gather_line(half, axis):
    rows = half.shape[0] // 2
    ahead, behind = shift(half, axis, 1), shift(half, axis, -1)
    low = shift(ahead[:rows], axis, 1)
    high = shift(behind[rows:], axis, -1)
    return [half, ahead, low, high, behind]


def line_rows(refs, column=slice(None)):
    own, ahead, low, high, behind = [ref[:, column] for ref in refs]
    return [own, ahead, jnp.concatenate([low, high], axis=0), behind]


def both_ways(a_blocks, b_blocks, a_axis, b_axis, sign):
    a_moved, b_moved = list(a_blocks), list(b_blocks)
    for k in (1, 3, 2):
        a_moved[k] = shift(a_blocks[k], a_axis, sign * k)
        b_moved[k] = shift(b_blocks[k], b_axis, sign * k)
    return a_moved, b_moved


def in_hbm(*arrays):
    return [pltpu.with_memory_space_constraint(array, pltpu.HBM) for array in arrays]


def prepare_kernel(token_ref, id_ref, gate_ref, a_ref, b_ref):
    tokens, depth = token_ref.shape
    half = depth // 2
    top = id_ref.shape[0]
    given = jnp.concatenate([id_ref[...].astype(jnp.float32), gate_ref[...]], axis=0).T
    lane = lax.broadcasted_iota(jnp.int32, (tokens, TILE), 1)
    number = lane.astype(jnp.float32)
    row = lax.broadcasted_iota(jnp.int32, (tokens, tokens), 0)
    column = lax.broadcasted_iota(jnp.int32, (tokens, tokens), 1)
    ids = [given[:, k : k + 1] for k in range(top)]
    named = jnp.zeros((tokens, TILE), jnp.float32)
    for k in range(top):
        named = jnp.where(ids[k] == number, 1.0, named)
    before = jnp.where(column < row, 1.0, 0.0).astype(jnp.bfloat16)
    rank = jnp.dot(before, named.astype(jnp.bfloat16), preferred_element_type=jnp.float32)
    facts = jnp.zeros((tokens, TILE), jnp.float32)
    for k in range(top):
        place = jnp.sum(jnp.where(ids[k] == number, rank, 0.0), axis=1, keepdims=True)
        facts = jnp.where(lane == k, ids[k], facts)
        facts = jnp.where(lane == top + k, place, facts)
        facts = jnp.where(lane == 2 * top + k, given[:, top + k : top + k + 1], facts)
    facts = facts.astype(jnp.bfloat16)
    a_ref[:, :half] = token_ref[:, :half]
    b_ref[:, :half] = token_ref[:, half:]
    a_ref[:, half:] = facts
    b_ref[:, half:] = facts


def prepare(tokens, expert_ids, gate_values):
    rows, depth = tokens.shape
    out = jax.ShapeDtypeStruct((rows, depth // 2 + TILE), jnp.bfloat16)
    top = expert_ids.shape[1]
    return pl.pallas_call(
        prepare_kernel,
        grid=(1,),
        in_specs=[
            pl.BlockSpec((rows, depth), lambda i: (0, 0)),
            pl.BlockSpec((top, rows), lambda i: (0, 0)),
            pl.BlockSpec((top, rows), lambda i: (0, 0)),
        ],
        out_specs=[pl.BlockSpec(out.shape, lambda i: (0, 0))] * 2,
        out_shape=[out, out],
        compiler_params=pltpu.CompilerParams(vmem_limit_bytes=VMEM),
        cost_estimate=pl.CostEstimate(
            flops=2 * rows * rows * TILE, bytes_accessed=4 * rows * depth, transcendentals=0
        ),
    )(*in_hbm(tokens, expert_ids.T, gate_values.T))


def codes(facts, top):
    facts = facts.astype(jnp.float32)
    return [facts[:, k : k + 1] * CAP + facts[:, top + k : top + k + 1] for k in range(top)]


def targets(experts_ref, first, chunks, tokens):
    count = len(chunks) * SIDE * ROWS
    lane = lax.broadcasted_iota(jnp.int32, (tokens, count), 1)
    code = jnp.zeros((tokens, count), jnp.int32)
    for n, chunk in enumerate(chunks):
        for dest in range(SIDE):
            low = (n * SIDE + dest) * ROWS
            value = experts_ref[first + dest] * CAP + chunk * ROWS + lane - low
            code = jnp.where((lane >= low) & (lane < low + ROWS), value, code)
    return code.astype(jnp.float32)


def pack_kernel(chunk, top, experts_ref, *refs):
    blocks, outs = refs[:-SIDE], refs[-SIDE:]
    tokens = blocks[0].shape[0]
    width = outs[0].shape[-1]
    target = targets(experts_ref, 0, (chunk,), tokens)
    facts = line_rows(blocks, slice(width, width + TILE))
    rows_in = line_rows(blocks, slice(0, width))
    for source in range(SIDE):
        pick = jnp.zeros(target.shape, jnp.float32)
        for code in codes(facts[source], top):
            pick = jnp.where(code == target, 1.0, pick)
        rows = jnp.dot(
            pick.T.astype(jnp.bfloat16), rows_in[source], preferred_element_type=jnp.float32
        ).astype(jnp.bfloat16)
        for dest in range(SIDE):
            outs[dest][source] = rows[dest * ROWS : (dest + 1) * ROWS]


def pack(chunk, top, experts, blocks):
    tokens, width = blocks[0].shape
    width -= TILE
    out = jax.ShapeDtypeStruct((SIDE, ROWS, width), jnp.bfloat16)
    return pl.pallas_call(
        functools.partial(pack_kernel, chunk, top),
        in_specs=[pl.BlockSpec(memory_space=pltpu.SMEM)]
        + [pl.BlockSpec(memory_space=pltpu.VMEM)] * len(blocks),
        out_specs=[pl.BlockSpec(memory_space=pltpu.VMEM)] * SIDE,
        out_shape=[out] * SIDE,
        compiler_params=pltpu.CompilerParams(vmem_limit_bytes=VMEM),
        cost_estimate=pl.CostEstimate(
            flops=2 * SIDE * SIDE * ROWS * tokens * width,
            bytes_accessed=2 * SIDE * width * (tokens + SIDE * ROWS),
            transcendentals=0,
        ),
    )(experts, *blocks)


def hidden_kernel(wg_ref, wu_ref, *refs):
    a_in, b_in = refs[:SIDE], refs[SIDE : 2 * SIDE]
    hidden_ref, x_ref, sems = refs[2 * SIDE :]
    half = x_ref.shape[-1] // 2
    count = SIDE * SIDE * ROWS

    @pl.when(pl.program_id(0) == 0)
    def _():
        copies = []
        for k in range(SIDE):
            copies.append(
                pltpu.make_async_copy(a_in[k], x_ref.at[:, k, :, :half], sems.at[k])
            )
            copies.append(
                pltpu.make_async_copy(b_in[k], x_ref.at[k, :, :, half:], sems.at[SIDE + k])
            )
        for copy in copies:
            copy.start()
        for copy in copies:
            copy.wait()

    x = x_ref[...].reshape(count, 2 * half)
    gate = jnp.dot(x, wg_ref[...], preferred_element_type=jnp.float32)
    up = jnp.dot(x, wu_ref[...], preferred_element_type=jnp.float32)
    hidden_ref[...] = (gate / (1.0 + jnp.exp(-gate)) * up).astype(jnp.bfloat16)


def hidden_rows(w_gate, w_up, a_in, b_in):
    depth, ff = w_gate.shape
    count = SIDE * SIDE * ROWS
    weight = pl.BlockSpec((depth, FF_TILE), lambda i: (0, i))
    return pl.pallas_call(
        hidden_kernel,
        grid=(ff // FF_TILE,),
        in_specs=[weight, weight] + [pl.BlockSpec(memory_space=pl.ANY)] * (2 * SIDE),
        out_specs=pl.BlockSpec((count, FF_TILE), lambda i: (0, i)),
        out_shape=jax.ShapeDtypeStruct((count, ff), jnp.bfloat16),
        scratch_shapes=[
            pltpu.VMEM((SIDE, SIDE, ROWS, depth), jnp.bfloat16),
            pltpu.SemaphoreType.DMA((2 * SIDE,)),
        ],
        compiler_params=pltpu.CompilerParams(vmem_limit_bytes=VMEM),
        cost_estimate=pl.CostEstimate(
            flops=4 * count * depth * ff,
            bytes_accessed=4 * depth * ff + 2 * count * depth,
            transcendentals=count * ff,
        ),
    )(w_gate, w_up, *a_in, *b_in)


def down_kernel(n_half, hidden_ref, wd_ref, *refs):
    a_out, b_out = refs[:SIDE], refs[SIDE:]
    out = jnp.dot(hidden_ref[...], wd_ref[...], preferred_element_type=jnp.float32)
    out = out.astype(jnp.bfloat16).reshape(SIDE, SIDE, ROWS, out.shape[1])

    @pl.when(pl.program_id(0) < n_half)
    def _():
        for k in range(SIDE):
            a_out[k][...] = out[:, k]

    @pl.when(pl.program_id(0) >= n_half)
    def _():
        for k in range(SIDE):
            b_out[k][...] = out[k]


def down_rows(hidden, w_down):
    count, ff = hidden.shape
    half = w_down.shape[1] // 2
    tile = min(D_TILE, half)
    n_half = half // tile
    a_spec = pl.BlockSpec((SIDE, ROWS, tile), lambda i: (0, 0, jnp.minimum(i, n_half - 1)))
    b_spec = pl.BlockSpec((SIDE, ROWS, tile), lambda i: (0, 0, jnp.maximum(i - n_half, 0)))
    out = jax.ShapeDtypeStruct((SIDE, ROWS, half), jnp.bfloat16)
    done = pl.pallas_call(
        functools.partial(down_kernel, n_half),
        grid=(2 * n_half,),
        in_specs=[
            pl.BlockSpec((count, ff), lambda i: (0, 0)),
            pl.BlockSpec((ff, tile), lambda i: (0, i)),
        ],
        out_specs=[a_spec] * SIDE + [b_spec] * SIDE,
        out_shape=[out] * (2 * SIDE),
        compiler_params=pltpu.CompilerParams(vmem_limit_bytes=VMEM),
        cost_estimate=pl.CostEstimate(
            flops=4 * count * half * ff,
            bytes_accessed=4 * half * ff + 4 * count * half,
            transcendentals=0,
        ),
    )(hidden, w_down)
    return done[:SIDE], done[SIDE:]


def sum_kernel(top, counts, experts_ref, *refs):
    groups = []
    for count in counts:
        groups.append(refs[:count])
        refs = refs[count:]
    a_in, b_in, a_facts, b_facts, a_out, b_out = groups
    tokens = a_out[0].shape[0]
    for first, ins, blocks, outs in ((0, a_in, a_facts, a_out), (SIDE, b_in, b_facts, b_out)):
        target = targets(experts_ref, first, tuple(range(CHUNKS)), tokens)
        facts = line_rows(blocks)
        for source in range(SIDE):
            wide = facts[source].astype(jnp.float32)
            weight = jnp.zeros(target.shape, jnp.float32)
            for k, code in enumerate(codes(wide, top)):
                gate = wide[:, 2 * top + k : 2 * top + k + 1]
                weight = jnp.where(code == target, gate, weight)
            rows = jnp.concatenate([ref[source] for ref in ins], axis=0)
            total = jnp.dot(
                weight.astype(jnp.bfloat16), rows, preferred_element_type=jnp.float32
            )
            if first:
                outs[0][experts_ref[2 * SIDE + source]] = total.astype(jnp.bfloat16)
            else:
                outs[source][...] = total.astype(jnp.bfloat16)


def sum_rows(top, experts, a_facts, b_facts, a_blocks, b_blocks):
    width = a_blocks[0].shape[-1]
    tokens = a_facts[0].shape[0]
    facts = [*a_facts, *b_facts]
    last = width // TILE
    whole = pl.BlockSpec(memory_space=pltpu.VMEM)
    out = pltpu.HBM((tokens, width), jnp.bfloat16)
    counts = (len(a_blocks), len(b_blocks), len(a_facts), len(b_facts), SIDE, 1)
    line = pltpu.HBM((SIDE, tokens, width), jnp.bfloat16)
    done = pl.pallas_call(
        functools.partial(sum_kernel, top, counts),
        grid=(1,),
        in_specs=[pl.BlockSpec(memory_space=pltpu.SMEM)]
        + [whole] * (len(a_blocks) + len(b_blocks))
        + [pl.BlockSpec((f.shape[0], TILE), lambda i: (0, last)) for f in facts],
        out_specs=[pl.BlockSpec(out.shape, lambda i: (0, 0))] * SIDE
        + [pl.BlockSpec(line.shape, lambda i: (0, 0, 0))],
        out_shape=[out] * SIDE + [line],
        compiler_params=pltpu.CompilerParams(vmem_limit_bytes=VMEM),
        cost_estimate=pl.CostEstimate(
            flops=4 * SIDE * SIDE * CAP * tokens * width,
            bytes_accessed=4 * SIDE * width * (tokens + SIDE * CAP),
            transcendentals=0,
        ),
    )(experts, *a_blocks, *b_blocks, *facts)
    return done[:SIDE], done[SIDE]


def local(tokens, expert_ids, gate_values, gate_weight, up_weight, down_weight):
    top = expert_ids.shape[1]
    z, x = lax.axis_index("z"), lax.axis_index("x")
    steps = jnp.arange(SIDE, dtype=jnp.int32)
    a_experts = z * SIDE + (x + steps) % SIDE
    b_experts = (z + steps) % SIDE * SIDE + x

    a_half, b_half = prepare(tokens, expert_ids, gate_values)
    b_rows = gather_line(b_half, "x")
    a_rows = gather_line(a_half, "z")

    w_gate, w_up, w_down = in_hbm(gate_weight[0], up_weight[0], down_weight[0])
    a_back, b_back = [], []
    for chunk in range(CHUNKS):
        a_out = list(pack(chunk, top, a_experts, a_rows))
        b_out = list(pack(chunk, top, b_experts, b_rows))
        a_experts, b_experts, a_out, b_out = lax.optimization_barrier(
            (a_experts, b_experts, a_out, b_out)
        )
        if chunk:
            b_out[2], hidden = lax.optimization_barrier((b_out[2], hidden))
            a_done, b_done = down_rows(hidden, w_down)
            a_home, b_home = both_ways(a_done, b_done, "x", "z", -1)
            a_back += a_home
            b_back += b_home
        a_in, b_in = both_ways(a_out, b_out, "x", "z", 1)
        hidden = hidden_rows(w_gate, w_up, a_in, b_in)
    hidden, a_back[1], a_back[3] = lax.optimization_barrier(
        (hidden, a_back[1], a_back[3])
    )
    a_done, b_done = down_rows(hidden, w_down)
    a_home, b_home = both_ways(a_done, b_done, "x", "z", -1)
    a_back += a_home
    b_back += b_home

    experts = jnp.concatenate([a_experts, b_experts, (x - steps) % SIDE])
    a_sums, b_sums = sum_rows(top, experts, a_rows, b_rows, a_back, b_back)
    b_home = lax.all_to_all(b_sums, "x", 0, 0, tiled=True)
    a_home = [a_sums[0]] + [shift(a_sums[k], "z", -k) for k in range(1, SIDE)]
    a_mixed = sum(part.astype(jnp.float32) for part in a_home)
    b_mixed = jnp.sum(b_home.astype(jnp.float32), axis=0)
    return jnp.concatenate([a_mixed, b_mixed], axis=1).astype(jnp.bfloat16)


def solution(mesh):
    dp = mesh.devices.shape[0]
    grid = Mesh(mesh.devices.reshape(dp, SIDE, SIDE), ("dp", "z", "x"))
    rows, experts = ("dp", "z", "x"), ("z", "x")
    in_specs = (
        P(rows, None),
        P(rows, None),
        P(rows, None),
        P(experts, None, None),
        P(experts, None, None),
        P(experts, None, None),
    )
    return jax.shard_map(
        local, mesh=grid, in_specs=in_specs, out_specs=P(rows, None), check_vma=False
    )
```
